512 devices in a mesh: height: 16 (over x, y_lo, core), width: 16 (over z), head: 2 (over y_hi).
Axes of the slice: x: 4, y: 4 (y_hi: 2, y_lo: 2; y = y_hi * 2 + y_lo), z: 16, core: 2. Of those that a mesh axis runs over, the one named last changes fastest.
Arguments:
- tokens: bfloat16 [16, 32, 144, 1536], P('height', 'width'), may hold values from -6 to 6
- grad_out: bfloat16 [16, 32, 144, 1536], P('height', 'width'), may hold values from -6 to 6
- qkv_weight: bfloat16 [1536, 3, 768], P(('height', 'width'), None, 'head'), may hold values from -0.15625 to 0.15625
- out_weight: bfloat16 [1536, 768], P(('height', 'width'), 'head'), may hold values from -0.5 to 0.5
- q_gain: float32 [768], P('head'), may hold values from 0.5 to 2
- k_gain: float32 [768], P('head'), may hold values from 0.5 to 2
- key_valid: int32 [16, 32, 144], P('height', 'width'), may hold values from 0 to 1, as said below
Outputs:
- mixed: bfloat16 [16, 32, 144, 1536], P('height', 'width', None, 'head')
- grad_in: bfloat16 [16, 32, 144, 1536], P('height', 'width', None, 'head')
The draws below stay inside these ranges and needn't reach their ends.
Inputs may be any that keep to these rules, and one draw needn't show every extreme that they name: key_valid is 0 only in the last row of tiles and in the last column of tiles. In a tile of the last row, each frame and column within the tile has its own count of valid rows, 1 to 5, and the rows from that count on are 0. In a tile of the last column, each frame and row within the tile has its own count of valid columns, 1 to 8, and the columns from that count on are 0. The first token of every tile is valid.
All inputs are finite; a program needn't handle non-finite values.
Results may differ from the reference program's by a relative error of at most 0.015.
Values may be sent and summed in bfloat16 or wider, within the bound.
No kernel may reach another device: no remote copies, remote signals or barrier semaphores. Data moves between devices by JAX's collectives and lax.ppermute only.
A program may use at most 128 MiB of HBM per device.

```python
import math
import jax
import jax.numpy as jnp
from jax import lax

D = 1536
HEAD_DIM = 128
HEADS = 6
FRAMES = 3
TILE_ROWS = 6
TILE_COLS = 8
TILE_TOK = 144
TILES_H = 16
TILES_W = 32
N_HEAD = 2


def draw_key_valid(key, part):
    key = jax.random.fold_in(key, 11)
    row_key, col_key = jax.random.split(key)
    row_counts = jax.random.randint(row_key, (TILES_W, FRAMES, TILE_COLS), 1, TILE_ROWS)
    col_counts = jax.random.randint(col_key, (TILES_H, FRAMES, TILE_ROWS), 1, TILE_COLS + 1)
    within = jnp.arange(TILE_TOK)
    frame_index = within // (TILE_ROWS * TILE_COLS)
    grid_row = within // TILE_COLS % TILE_ROWS
    grid_col = within % TILE_COLS
    row_limit = row_counts[:, frame_index, grid_col].reshape(1, TILES_W, TILE_TOK)
    col_limit = col_counts[:, frame_index, grid_row].reshape(TILES_H, 1, TILE_TOK)
    tile_row = jnp.arange(TILES_H).reshape(-1, 1, 1)
    tile_col = jnp.arange(TILES_W).reshape(1, -1, 1)
    row_pad = (tile_row == TILES_H - 1) & (grid_row.reshape(1, 1, -1) >= row_limit)
    col_pad = (tile_col == TILES_W - 1) & (grid_col.reshape(1, 1, -1) >= col_limit)
    return jnp.where(row_pad | col_pad, 0, 1).astype(jnp.int32)


def block_scale(own_key, extent, pieces, low, high):
    def one(axis_at, blocks):
        heights = jax.random.uniform(jax.random.fold_in(jax.random.fold_in(own_key, 6), axis_at), (blocks,), jnp.float32, low / len(pieces), high / len(pieces))
        return jnp.repeat(jnp.exp(heights), extent[axis_at] // blocks).reshape((-1,) + (1,) * (len(extent) - axis_at - 1))

    level = one(*pieces[0])
    for cut in pieces[1:]:
        level = level * one(*cut)
    return level


def centred(key, dims, deviation, reach, shards=(), dtype=jnp.bfloat16):
    entries = jax.random.normal(key, dims, jnp.float32) * deviation
    if len(shards) > 0:
        entries = block_scale(key, dims, shards, -0.22, 0.18) * entries
    return jnp.clip(entries, min=-reach, max=reach).astype(dtype)


def setup_inputs(seed: int = 0) -> dict:
    keys = jax.random.split(jax.random.key(seed), 8)
    tokens = centred(keys[0], (TILES_H, TILES_W, TILE_TOK, D), 1.0, 6.0, ((0, 16), (1, 16)))
    grad_out = centred(keys[1], (TILES_H, TILES_W, TILE_TOK, D), 1.0, 6.0, ((0, 16), (1, 16)))
    qkv_weight = centred(keys[2], (D, 3, HEADS * HEAD_DIM), D ** -0.5, 0.15625, ((0, 256), (2, 2)))
    out_weight = centred(keys[3], (D, HEADS * HEAD_DIM), HEAD_DIM ** -0.5, 0.5, ((0, 256), (1, 2)))
    q_gain = jnp.clip(jnp.exp(math.log(2.0) - 1.3862944 * jax.random.uniform(keys[4], (HEADS * HEAD_DIM,), jnp.float32) ** block_scale(keys[4], (HEADS * HEAD_DIM,), ((0, 2),), -0.2, 0.2)), 0.5, 2.0)
    k_gain = jnp.clip(jnp.exp(math.log(2.0) - 1.3862944 * jax.random.uniform(keys[5], (HEADS * HEAD_DIM,), jnp.float32) ** block_scale(keys[5], (HEADS * HEAD_DIM,), ((0, 2),), -0.2, 0.2)), 0.5, 2.0)
    key_valid = draw_key_valid(jax.random.fold_in(keys[7], 71), 0)
    return {"tokens": tokens, "grad_out": grad_out, "qkv_weight": qkv_weight, "out_weight": out_weight, "q_gain": q_gain, "k_gain": k_gain, "key_valid": key_valid}


epsilon = 1e-06

def norm_scale(raw_values, gain_vec):
    inverse = lax.rsqrt(lax.optimization_barrier(jnp.mean(raw_values * raw_values, axis=-1, keepdims=True)) + epsilon)
    return (raw_values * inverse * gain_vec, inverse)

def norm_backward(raw_values, inverse, gain_vec, upstream):
    weighted = gain_vec * upstream
    inner_mean = lax.optimization_barrier(jnp.mean(weighted * raw_values, axis=-1, keepdims=True))
    return inverse * weighted - raw_values * inverse ** 3 * inner_mean

def windows(extended, tile_rows, tile_cols):
    return jnp.stack([extended[row_step:row_step + tile_rows, col_step:col_step + tile_cols] for row_step in range(3) for col_step in range(3)], axis=2)

def fold_windows(windowed, tile_rows, tile_cols):
    total = jnp.zeros((tile_rows + 2, tile_cols + 2) + windowed.shape[3:], jnp.float32)
    for position in range(9):
        row_step, col_step = divmod(position, 3)
        total = total.at[row_step:row_step + tile_rows, col_step:col_step + tile_cols].add(windowed[:, :, position])
    return total

def attend(queries, win_keys, win_values, win_valid, upstream):
    factor = HEAD_DIM ** (-0.5)
    query_f = queries.astype(jnp.float32)
    keys_f = win_keys.astype(jnp.float32)
    values_f = win_values.astype(jnp.float32)
    upstream_f = upstream.astype(jnp.float32)
    scores = jnp.einsum('bqhe,bkhe->bhqk', query_f, keys_f) * factor
    weights = jnp.exp(scores) * win_valid[:, None, None, :]
    attn_probs = weights / lax.optimization_barrier(jnp.sum(weights, axis=-1, keepdims=True))
    attn_weights = attn_probs.astype(jnp.bfloat16).astype(jnp.float32)
    attended = jnp.einsum('bhqk,bkhe->bqhe', attn_weights, values_f).astype(jnp.bfloat16)
    grad_probs = jnp.einsum('bqhe,bkhe->bhqk', upstream_f, values_f)
    grad_scores = attn_probs * (grad_probs - lax.optimization_barrier(jnp.sum(attn_probs * grad_probs, axis=-1, keepdims=True)))
    grad_scores = grad_scores.astype(jnp.bfloat16).astype(jnp.float32)
    grad_values = jnp.einsum('bhqk,bqhe->bkhe', attn_weights, upstream_f)
    grad_keys = jnp.einsum('bhqk,bqhe->bkhe', grad_scores, query_f) * factor
    grad_queries = jnp.einsum('bhqk,bkhe->bqhe', grad_scores, keys_f) * factor
    return (attended, grad_queries, grad_keys, grad_values)

def rounded(values):
    return lax.optimization_barrier(values.astype(jnp.bfloat16)).astype(jnp.float32)

def group_sum(left, right, group_count, inner_width):
    total = jnp.zeros((left.shape[0], right.shape[0]), jnp.float32)
    for group_index in range(group_count):
        left_part = left[:, :, group_index * inner_width:(group_index + 1) * inner_width].reshape(left.shape[0], -1)
        right_part = right[:, :, group_index * inner_width:(group_index + 1) * inner_width].reshape(right.shape[0], -1)
        total = total + rounded(jnp.dot(left_part, right_part.T, preferred_element_type=jnp.float32))
    return total.astype(jnp.bfloat16)

def reference(tokens, grad_out, qkv_weight, out_weight, q_gain, k_gain, key_valid):
    head_count = q_gain.shape[0] // HEAD_DIM
    all_inner = head_count * HEAD_DIM
    token_rows = tokens.reshape(-1, D)
    token_count = token_rows.shape[0]
    projected = jnp.dot(token_rows, qkv_weight.reshape(D, 3 * all_inner), preferred_element_type=jnp.float32)
    projected = projected.reshape(token_count, 3, head_count, HEAD_DIM)
    q_raw = projected[:, 0]
    k_raw = projected[:, 1]
    v_raw = projected[:, 2]
    q_gains = q_gain.reshape(head_count, HEAD_DIM)
    k_gains = k_gain.reshape(head_count, HEAD_DIM)
    q_normed, q_inverse = norm_scale(q_raw, q_gains)
    k_normed, k_inverse = norm_scale(k_raw, k_gains)
    shape_tiles = (TILES_H, TILES_W, TILE_TOK, head_count, HEAD_DIM)
    queries = q_normed.astype(jnp.bfloat16).reshape(shape_tiles)
    keys_tiled = k_normed.astype(jnp.bfloat16).reshape(shape_tiles)
    values_tiled = v_raw.astype(jnp.bfloat16).reshape(shape_tiles)
    border = ((1, 1), (1, 1), (0, 0), (0, 0), (0, 0))
    win_keys = windows(jnp.pad(keys_tiled, border), TILES_H, TILES_W).reshape(TILES_H, TILES_W, 9 * TILE_TOK, head_count, HEAD_DIM)
    win_values = windows(jnp.pad(values_tiled, border), TILES_H, TILES_W).reshape(TILES_H, TILES_W, 9 * TILE_TOK, head_count, HEAD_DIM)
    valid_ext = jnp.pad(key_valid.astype(jnp.float32), ((1, 1), (1, 1), (0, 0)))
    win_valid = windows(valid_ext, TILES_H, TILES_W).reshape(TILES_H, TILES_W, 9 * TILE_TOK)
    grad_attended = jnp.dot(grad_out.reshape(-1, D), out_weight, preferred_element_type=jnp.float32)
    grad_attended = grad_attended.astype(jnp.bfloat16).reshape(shape_tiles)

    def one_row(items):
        return attend(*items)
    attended, grad_queries, grad_keys_win, grad_values_win = lax.map(one_row, (queries, win_keys, win_values, win_valid, grad_attended))
    win_shape = (TILES_H, TILES_W, 9, TILE_TOK, head_count, HEAD_DIM)
    grad_keys = fold_windows(grad_keys_win.reshape(win_shape), TILES_H, TILES_W)[1:-1, 1:-1]
    grad_values = fold_windows(grad_values_win.reshape(win_shape), TILES_H, TILES_W)[1:-1, 1:-1]
    grad_q_raw = norm_backward(q_raw, q_inverse, q_gains, grad_queries.reshape(token_count, head_count, HEAD_DIM))
    grad_k_raw = norm_backward(k_raw, k_inverse, k_gains, grad_keys.reshape(token_count, head_count, HEAD_DIM))
    grad_qkv = jnp.stack([grad_q_raw, grad_k_raw, grad_values.reshape(token_count, head_count, HEAD_DIM)], axis=1)
    grad_qkv = grad_qkv.reshape(token_count, 3, all_inner).astype(jnp.bfloat16)
    inner_width = all_inner // N_HEAD
    mixed = group_sum(attended.reshape(token_count, 1, all_inner), out_weight.reshape(D, 1, all_inner), N_HEAD, inner_width)
    grad_in = group_sum(grad_qkv, qkv_weight, N_HEAD, inner_width)
    out_shape = (TILES_H, TILES_W, TILE_TOK, D)
    return (mixed.reshape(out_shape), grad_in.reshape(out_shape))
```

```python
import jax
import jax.numpy as jnp
from jax import lax
from jax.sharding import PartitionSpec as P

HEAD_DIM = 128


epsilon = 1e-06


def padded(x, sides, width):
    for axis, dim in sides:
        count, length = (lax.axis_size(axis), x.shape[dim])
        up = [(i, (i + 1) % count) for i in range(count - 1)]
        down = [(j, i) for i, j in up]
        last = lax.slice_in_dim(x, length - width, length, axis=dim)
        first = lax.slice_in_dim(x, 0, width, axis=dim)
        before = lax.ppermute(last, axis, up)
        after = lax.ppermute(first, axis, down)
        x = jnp.concatenate([before, x, after], axis=dim)
    return x


def norm_scale(raw_values, gain_vec):
    inverse = lax.rsqrt(jnp.mean(raw_values * raw_values, axis=-1, keepdims=True) + epsilon)
    return (raw_values * inverse * gain_vec, inverse)


def norm_backward(raw_values, inverse, gain_vec, upstream):
    weighted = gain_vec * upstream
    inner_mean = jnp.mean(weighted * raw_values, axis=-1, keepdims=True)
    return inverse * weighted - raw_values * inverse**3 * inner_mean


def windows(extended, tile_rows, tile_cols):
    return jnp.stack(
        [
            extended[row_step : row_step + tile_rows, col_step : col_step + tile_cols]
            for row_step in range(3)
            for col_step in range(3)
        ],
        axis=2,
    )


def fold_windows(windowed, tile_rows, tile_cols):
    total = jnp.zeros((tile_rows + 2, tile_cols + 2) + windowed.shape[3:], jnp.float32)
    for position in range(9):
        row_step, col_step = divmod(position, 3)
        total = total.at[row_step : row_step + tile_rows, col_step : col_step + tile_cols].add(
            windowed[:, :, position]
        )
    return total


def fold_along(values, along, length):
    middle = lax.slice_in_dim(values, 2, length + 2, axis=along)
    first_rim = lax.slice_in_dim(values, 0, 1, axis=along)
    last_rim = lax.slice_in_dim(values, length + 3, length + 4, axis=along)
    before = [(0, 0)] * values.ndim
    before[along] = (0, length - 1)
    behind = [(0, 0)] * values.ndim
    behind[along] = (length - 1, 0)
    return middle + jnp.pad(first_rim, before) + jnp.pad(last_rim, behind)


def attend(queries, win_keys, win_values, win_valid, upstream):
    factor = HEAD_DIM ** (-0.5)
    scores = (
        jnp.einsum("bqhe,bkhe->bhqk", queries, win_keys, preferred_element_type=jnp.float32)
        * factor
    )
    weights = jnp.exp(scores) * win_valid[:, None, None, :]
    attn_probs = weights / jnp.sum(weights, axis=-1, keepdims=True)
    attn_weights = attn_probs.astype(jnp.bfloat16)
    attended = jnp.einsum(
        "bhqk,bkhe->bqhe", attn_weights, win_values, preferred_element_type=jnp.float32
    ).astype(jnp.bfloat16)
    grad_probs = jnp.einsum(
        "bqhe,bkhe->bhqk", upstream, win_values, preferred_element_type=jnp.float32
    )
    grad_scores = attn_probs * (
        grad_probs - jnp.sum(attn_probs * grad_probs, axis=-1, keepdims=True)
    )
    grad_scores = grad_scores.astype(jnp.bfloat16)
    grad_values = jnp.einsum(
        "bhqk,bqhe->bkhe", attn_weights, upstream, preferred_element_type=jnp.float32
    )
    grad_keys = (
        jnp.einsum("bhqk,bqhe->bkhe", grad_scores, queries, preferred_element_type=jnp.float32)
        * factor
    )
    grad_queries = (
        jnp.einsum("bhqk,bkhe->bqhe", grad_scores, win_keys, preferred_element_type=jnp.float32)
        * factor
    )
    return (attended, grad_queries, grad_keys, grad_values)


def on_device(tokens, grad_out, qkv_weight, out_weight, q_gain, k_gain, key_valid):
    tile_rows, tile_cols, tile_tokens, model_width = tokens.shape
    head_count = q_gain.shape[0] // HEAD_DIM
    inner_width = head_count * HEAD_DIM
    token_count = tile_rows * tile_cols * tile_tokens
    tile_count = tile_rows * tile_cols
    fan = 3 * inner_width
    shard_rows = qkv_weight.shape[0]
    joined = jnp.concatenate([qkv_weight.reshape(shard_rows, fan), out_weight], axis=1)
    along_width = lax.all_gather(joined, "width", axis=0, tiled=True)
    whole = lax.all_gather(along_width, "height", axis=0, tiled=True)
    whole_qkv, whole_out = whole[:, :fan], whole[:, fan:]
    projected = jnp.dot(
        tokens.reshape(token_count, model_width),
        whole_qkv.reshape(model_width, 3 * inner_width),
        preferred_element_type=jnp.float32,
    ).reshape(token_count, 3, head_count, HEAD_DIM)
    q_gains = q_gain.reshape(head_count, HEAD_DIM)
    k_gains = k_gain.reshape(head_count, HEAD_DIM)
    q_normed, q_inverse = norm_scale(projected[:, 0], q_gains)
    k_normed, k_inverse = norm_scale(projected[:, 1], k_gains)
    shape_tiles = (tile_rows, tile_cols, tile_tokens, head_count, HEAD_DIM)
    queries = q_normed.astype(jnp.bfloat16).reshape(tile_count, tile_tokens, head_count, HEAD_DIM)
    keys_tiled = k_normed.astype(jnp.bfloat16).reshape(shape_tiles)
    values_tiled = projected[:, 2].astype(jnp.bfloat16).reshape(shape_tiles)
    keys_ext, values_ext, valid_ext = (
        padded(keys_tiled, (("height", 0), ("width", 1)), 1),
        padded(values_tiled, (("height", 0), ("width", 1)), 1),
        padded(key_valid.astype(jnp.bfloat16), (("height", 0), ("width", 1)), 1),
    )
    win_keys = windows(keys_ext, tile_rows, tile_cols).reshape(
        tile_count, 9 * tile_tokens, head_count, HEAD_DIM
    )
    win_values = windows(values_ext, tile_rows, tile_cols).reshape(
        tile_count, 9 * tile_tokens, head_count, HEAD_DIM
    )
    win_valid = (
        windows(valid_ext, tile_rows, tile_cols)
        .reshape(tile_count, 9 * tile_tokens)
        .astype(jnp.float32)
    )
    grad_attended = jnp.dot(
        grad_out.reshape(token_count, model_width), whole_out, preferred_element_type=jnp.float32
    )
    grad_attended = grad_attended.astype(jnp.bfloat16).reshape(
        tile_count, tile_tokens, head_count, HEAD_DIM
    )
    attended, grad_queries, grad_keys_win, grad_values_win = attend(
        queries, win_keys, win_values, win_valid, grad_attended
    )
    win_shape = (tile_rows, tile_cols, 9, tile_tokens, head_count, HEAD_DIM)
    keys_back = fold_windows(grad_keys_win.reshape(win_shape), tile_rows, tile_cols)
    values_back = fold_windows(grad_values_win.reshape(win_shape), tile_rows, tile_cols)
    keys_recv, values_recv = (
        padded(keys_back.astype(jnp.bfloat16), (("height", 0), ("width", 1)), 1).astype(
            keys_back.dtype
        ),
        padded(values_back.astype(jnp.bfloat16), (("height", 0), ("width", 1)), 1).astype(
            values_back.dtype
        ),
    )
    grad_keys = fold_along(fold_along(keys_recv, 0, tile_rows), 1, tile_cols)
    grad_values = fold_along(fold_along(values_recv, 0, tile_rows), 1, tile_cols)
    grad_q_raw = norm_backward(
        projected[:, 0], q_inverse, q_gains, grad_queries.reshape(token_count, head_count, HEAD_DIM)
    )
    grad_k_raw = norm_backward(
        projected[:, 1], k_inverse, k_gains, grad_keys.reshape(token_count, head_count, HEAD_DIM)
    )
    grad_qkv = jnp.stack(
        [grad_q_raw, grad_k_raw, grad_values.reshape(token_count, head_count, HEAD_DIM)], axis=1
    )
    grad_qkv = grad_qkv.reshape(token_count, 3, inner_width).astype(jnp.bfloat16)
    attended_rows = attended.reshape(token_count, inner_width)
    mixed_part = jnp.dot(attended_rows, whole_out.T, preferred_element_type=jnp.float32)
    mixed = lax.psum_scatter(
        mixed_part.astype(jnp.bfloat16), "head", scatter_dimension=1, tiled=True
    )
    grad_part = jnp.dot(
        grad_qkv.reshape(token_count, 3 * inner_width),
        whole_qkv.reshape(model_width, 3 * inner_width).T,
        preferred_element_type=jnp.float32,
    )
    grad_in = lax.psum_scatter(
        grad_part.astype(jnp.bfloat16), "head", scatter_dimension=1, tiled=True
    )
    out_shape = (tile_rows, tile_cols, tile_tokens, -1)
    return (mixed.reshape(out_shape), grad_in.reshape(out_shape))


def solution(mesh):
    placed = (
        P("height", "width", None, None),
        P("height", "width", None, None),
        P(("height", "width"), None, "head"),
        P(("height", "width"), "head"),
        P("head"),
        P("head"),
        P("height", "width", None),
    )
    return jax.shard_map(
        on_device,
        mesh=mesh,
        in_specs=placed,
        out_specs=(P("height", "width", None, "head"), P("height", "width", None, "head")),
        check_vma=False,
    )
```

```python
import functools

import jax
import jax.numpy as jnp
from jax import lax
from jax.experimental import pallas as pl
from jax.experimental.pallas import tpu as pltpu
from jax.sharding import PartitionSpec as P

HEAD_DIM = 128
LANES = 128
TILE = 144
COLUMN = 3 * TILE
WINDOW = 9 * TILE
EXTENDED = 12 * TILE
OWN_TILES = (4, 7)
MASK_LANE = 18
MASK_DEPTH = 1e5
FACTOR = HEAD_DIM ** (-0.5)
VMEM_BYTES = 50 * 1024 * 1024
epsilon = 1e-06


def dot_rows(left, right):
    return lax.dot_general(left, right, (((1,), (1,)), ((), ())), preferred_element_type=jnp.float32)


def dot_plain(left, right):
    return jnp.dot(left, right, preferred_element_type=jnp.float32)


def lane_index(rows):
    return lax.broadcasted_iota(jnp.int32, (rows, LANES), 1)


def norm_inverse(raw_values):
    return lax.rsqrt(jnp.mean(raw_values * raw_values, axis=-1, keepdims=True) + epsilon)


def norm_backward(raw_values, gain_vec, upstream):
    inverse = norm_inverse(raw_values)
    weighted = gain_vec * upstream
    inner_mean = jnp.mean(weighted * raw_values, axis=-1, keepdims=True)
    return inverse * weighted - raw_values * (inverse * inverse * inverse) * inner_mean


def three_parts(values):
    first = values.astype(jnp.bfloat16)
    rest = values - first.astype(jnp.float32)
    second = rest.astype(jnp.bfloat16)
    third = (rest - second.astype(jnp.float32)).astype(jnp.bfloat16)
    return [part.astype(jnp.float32) for part in (first, second, third)]


def extended_copies(own, up, down, left, right, target, sems):
    tile = lambda ref, i: ref.at[pl.ds(i * TILE, TILE)]
    pairs = [
        (left, 0, 3),
        (tile(up, 0), 3, 1),
        (tile(own, 0), 4, 1),
        (tile(down, 0), 5, 1),
        (tile(up, 1), 6, 1),
        (tile(own, 1), 7, 1),
        (tile(down, 1), 8, 1),
        (right, 9, 3),
    ]
    return [
        pltpu.make_async_copy(src, target.at[pl.ds(at * TILE, count * TILE)], sems.at[n])
        for n, (src, at, count) in enumerate(pairs)
    ]


def front_kernel(place, own, up, down, left, right, upstream, *rest):
    blocks, rest = rest[:16], rest[16:]
    (q_gain, k_gain, whole, queries, own_keys, own_values, own_marks, own_k_raw, grad_q, attended,
     message, tok, grad, keys, values, marks, raw, token_sems, block_sems, grad_sem) = rest
    here = place[0]
    north, south = lax.rem(here + 12, 16), lax.rem(here + 4, 16)
    far = lax.rem(here + 8, 16)
    spots = [here, here ^ 2, north, south, north ^ 2, south ^ 2, far, far ^ 2]
    spots = spots + [spot ^ 1 for spot in spots]
    block_copies = [
        pltpu.make_async_copy(block, whole.at[pl.ds(pl.multiple_of(spot * 96, 96), 96)], block_sems.at[n])
        for n, (block, spot) in enumerate(zip(blocks, spots))
    ]
    grad_copy = pltpu.make_async_copy(upstream, grad, grad_sem.at[0])
    token_copies = extended_copies(own, up, down, left, right, tok, token_sems)
    for copy in block_copies + [grad_copy] + token_copies:
        copy.start()
    for copy in block_copies + [grad_copy]:
        copy.wait()
    heads = range(queries.shape[1] // HEAD_DIM)
    inner = queries.shape[1]
    model = whole.shape[0]
    message[:, :inner] = dot_plain(grad[...], whole[:, 3 * inner :]).astype(jnp.bfloat16)
    for copy in token_copies:
        copy.wait()
    chunk = 2 * TILE

    def project(step, carry):
        rows = pl.ds(pl.multiple_of(step * chunk, chunk), chunk)
        result = dot_plain(tok[rows, :model], whole[:, : 3 * inner])
        raw[rows, :] = result[:, : 2 * inner]
        for head in heads:
            lanes = slice(head * HEAD_DIM, (head + 1) * HEAD_DIM)
            q_raw = result[:, lanes]
            queries[rows, lanes] = (q_raw * norm_inverse(q_raw) * q_gain[:, lanes]).astype(jnp.bfloat16)
            k_raw = result[:, inner:][:, lanes]
            keys[rows, lanes] = (k_raw * norm_inverse(k_raw) * k_gain[:, lanes]).astype(jnp.bfloat16)
        values[rows, :] = result[:, 2 * inner :].astype(jnp.bfloat16)
        valid = tok[rows, model:].astype(jnp.float32)
        deep = jnp.where(lane_index(chunk) == MASK_LANE, MASK_DEPTH, 0.0)
        marks[rows, :] = (valid * deep - deep).astype(jnp.bfloat16)
        return carry

    lax.fori_loop(0, EXTENDED // chunk, project, 0)
    lane = lane_index(TILE)
    one_mark = jnp.where(lane == MASK_LANE, 1.0, 0.0)
    for tile, at in enumerate(OWN_TILES):
        mine = slice(tile * TILE, (tile + 1) * TILE)
        ext = slice(at * TILE, (at + 1) * TILE)
        window = slice(tile * COLUMN, tile * COLUMN + WINDOW)
        stats = one_mark
        for head in heads:
            lanes = slice(head * HEAD_DIM, (head + 1) * HEAD_DIM)
            q_aug = jnp.concatenate([queries[ext, lanes], one_mark.astype(jnp.bfloat16)], axis=1)
            win_keys = keys[window, lanes]
            win_values = values[window, lanes]
            k_aug = jnp.concatenate([win_keys, marks[window, :]], axis=1)
            weights = jnp.exp(dot_rows(q_aug, k_aug) * FACTOR)
            total = jnp.sum(weights, axis=-1, keepdims=True)
            probs = weights * (1.0 / total)
            attended[mine, lanes] = dot_plain(probs.astype(jnp.bfloat16), win_values).astype(jnp.bfloat16)
            grad_probs = dot_rows(message[mine, lanes], win_values)
            delta = jnp.sum(probs * grad_probs, axis=-1, keepdims=True)
            grad_scores = (probs * (grad_probs - delta)).astype(jnp.bfloat16)
            upstream_q = dot_plain(grad_scores, win_keys) * FACTOR
            grad_q[mine, lanes] = norm_backward(raw[ext, lanes], q_gain[:, lanes], upstream_q).astype(jnp.bfloat16)
            for n, part in enumerate(three_parts(jnp.log(total) * (1.0 / FACTOR))):
                stats = jnp.where(lane == 3 * head + n, part, stats)
            for n, part in enumerate(three_parts(delta)):
                stats = jnp.where(lane == 9 + 3 * head + n, part, stats)
        message[mine, inner:] = stats.astype(jnp.bfloat16)
        own_keys[mine, :] = keys[ext, :]
        own_values[mine, :] = values[ext, :]
        own_marks[mine, :] = marks[ext, :]
        own_k_raw[mine, :] = raw[ext, inner:]


def back_kernel(place, own, up, down, left, right, queries, keys, values, marks, k_raw, grad_q, whole, k_gain,
                kept, sent, ext, grad_qkv, sems):
    copies = extended_copies(own, up, down, left, right, ext, sems)
    for copy in copies:
        copy.start()
    for copy in copies:
        copy.wait()
    inner = queries.shape[1]
    grad_qkv[:, :inner] = grad_q[...]
    lane = lane_index(TILE)
    for tile in range(2):
        mine = slice(tile * TILE, (tile + 1) * TILE)
        window = slice(tile * COLUMN, tile * COLUMN + WINDOW)
        stats = ext[window, inner:]
        for head in range(inner // HEAD_DIM):
            lanes = slice(head * HEAD_DIM, (head + 1) * HEAD_DIM)
            k_signs = jnp.where((lane >= 3 * head) & (lane < 3 * head + 3), -1.0, 0.0).astype(jnp.bfloat16)
            v_signs = jnp.where((lane >= 9 + 3 * head) & (lane < 12 + 3 * head), -1.0, 0.0).astype(jnp.bfloat16)
            k_aug = jnp.concatenate([keys[mine, lanes], marks[mine, :] + k_signs], axis=1)
            v_aug = jnp.concatenate([values[mine, lanes], v_signs], axis=1)
            win_queries = queries[window, lanes]
            win_upstream = ext[window, lanes]
            probs = jnp.exp(dot_rows(k_aug, jnp.concatenate([win_queries, stats], axis=1)) * FACTOR)
            centred = dot_rows(v_aug, jnp.concatenate([win_upstream, stats], axis=1))
            grad_scores = (probs * centred).astype(jnp.bfloat16)
            grad_v = dot_plain(probs.astype(jnp.bfloat16), win_upstream)
            upstream_k = dot_plain(grad_scores, win_queries) * FACTOR
            grad_k = norm_backward(k_raw[mine, lanes], k_gain[:, lanes], upstream_k)
            grad_qkv[mine, inner + head * HEAD_DIM : inner + (head + 1) * HEAD_DIM] = grad_k.astype(jnp.bfloat16)
            grad_qkv[mine, 2 * inner + head * HEAD_DIM : 2 * inner + (head + 1) * HEAD_DIM] = grad_v.astype(jnp.bfloat16)
    half = kept.shape[1]
    for target, group in ((sent, 1 - place[1]), (kept, place[1])):
        rows = pl.ds(pl.multiple_of(group * half, half), half)
        target[...] = dot_rows(grad_qkv[...], whole[rows, : 3 * inner]).astype(jnp.bfloat16)


def steps(axis, shift, wrap=False):
    count = lax.axis_size(axis)
    return [(i, (i + shift) % count) for i in range(count) if wrap or 0 <= i + shift < count]


def spread_height(own):
    up = lax.ppermute(own, "height", steps("height", 1))
    down = lax.ppermute(own, "height", steps("height", -1))
    return up, down


def spread_width(own, up, down):
    column = lambda i: jnp.concatenate([part[i * TILE : (i + 1) * TILE] for part in (up, own, down)], axis=0)
    left = lax.ppermute(column(1), "width", steps("width", 1))
    right = lax.ppermute(column(0), "width", steps("width", -1))
    return left, right


def flip(x, bit):
    count = lax.axis_size("height")
    return lax.ppermute(x, "height", [(i, i ^ bit) for i in range(count)])


def gather_height(block):
    shift = lambda x, by: lax.ppermute(x, "height", steps("height", by, True))
    rows = block.shape[0]
    north, south = shift(block, 4), shift(block, -4)
    beside = flip(block, 2)
    north_beside, south_beside = shift(beside, 4), shift(beside, -4)
    far, far_beside = shift(north, 4), shift(south_beside, -4)
    mine = [block, beside, north, south, north_beside, south_beside, far, far_beside]
    groups = [mine[:2], mine[2:6], mine[6:]]
    other = []
    for group in groups:
        swapped = flip(jnp.concatenate(group, axis=0), 1)
        other += [swapped[n * rows : (n + 1) * rows] for n in range(len(group))]
    return mine + other


def whole_spec():
    return pl.BlockSpec(memory_space=pltpu.VMEM)


def on_device(tokens, grad_out, qkv_weight, out_weight, q_gain, k_gain, key_valid):
    model = tokens.shape[-1]
    inner = q_gain.shape[0]
    count = tokens.shape[0] * tokens.shape[1] * tokens.shape[2]
    shard_rows = qkv_weight.shape[0]
    place = jnp.stack([lax.axis_index("height"), lax.axis_index("head")]).astype(jnp.int32)
    valid = key_valid.reshape(count, 1).astype(jnp.bfloat16)
    marked = jnp.concatenate([tokens.reshape(count, model), jnp.broadcast_to(valid, (count, LANES))], axis=1)
    up, down = spread_height(marked)
    joined = jnp.concatenate([qkv_weight.reshape(shard_rows, 3 * inner), out_weight], axis=1)
    along_width = lax.all_gather(joined, "width", axis=0, tiled=True)
    left, right = spread_width(marked, up, down)
    blocks = gather_height(along_width)
    q_gains, k_gains = q_gain.reshape(1, inner), k_gain.reshape(1, inner)
    anywhere = pl.BlockSpec(memory_space=pl.ANY)
    shape = jax.ShapeDtypeStruct
    half = jnp.bfloat16
    whole, queries, keys, values, marks, k_raw, grad_q, attended, message = pl.pallas_call(
        front_kernel,
        out_shape=(
            shape((model, 4 * inner), half),
            shape((EXTENDED, inner), half),
            shape((count, inner), half),
            shape((count, inner), half),
            shape((count, LANES), half),
            shape((count, inner), jnp.float32),
            shape((count, inner), half),
            shape((count, inner), half),
            shape((count, inner + LANES), half),
        ),
        in_specs=[pl.BlockSpec(memory_space=pltpu.SMEM)] + [anywhere] * 22 + [whole_spec()] * 2,
        out_specs=tuple(whole_spec() for _ in range(9)),
        scratch_shapes=[
            pltpu.VMEM((EXTENDED, model + LANES), half),
            pltpu.VMEM((count, model), half),
            pltpu.VMEM((EXTENDED, inner), half),
            pltpu.VMEM((EXTENDED, inner), half),
            pltpu.VMEM((EXTENDED, LANES), half),
            pltpu.VMEM((EXTENDED, 2 * inner), jnp.float32),
            pltpu.SemaphoreType.DMA((8,)),
            pltpu.SemaphoreType.DMA((16,)),
            pltpu.SemaphoreType.DMA((1,)),
        ],
        compiler_params=pltpu.CompilerParams(vmem_limit_bytes=VMEM_BYTES),
        name="front",
    )(place, marked, up, down, left, right, grad_out.reshape(count, model), *blocks, q_gains, k_gains)

    group = lax.axis_index("head")
    width = model // 2
    swap = lambda x: lax.ppermute(x, "head", [(0, 1), (1, 0)])
    part = lambda which: lax.dynamic_slice(whole, (which * width, 3 * inner), (width, inner))
    up, down = spread_height(message)
    mixed_sent = dot_rows(attended, part(1 - group)).astype(half)
    mixed_kept = dot_rows(attended, part(group)).astype(half)
    mixed_got = swap(mixed_sent)
    left, right = spread_width(message, up, down)
    kept, sent = pl.pallas_call(
        back_kernel,
        out_shape=(shape((count, width), half), shape((count, width), half)),
        in_specs=[pl.BlockSpec(memory_space=pltpu.SMEM)] + [anywhere] * 5 + [whole_spec()] * 8,
        out_specs=(whole_spec(), whole_spec()),
        scratch_shapes=[
            pltpu.VMEM((EXTENDED, inner + LANES), half),
            pltpu.VMEM((count, 3 * inner), half),
            pltpu.SemaphoreType.DMA((8,)),
        ],
        compiler_params=pltpu.CompilerParams(vmem_limit_bytes=VMEM_BYTES),
        name="back",
    )(place, message, up, down, left, right, queries, keys, values, marks, k_raw, grad_q, whole, k_gains)
    total = lambda a, b: (a.astype(jnp.float32) + b.astype(jnp.float32)).astype(half)
    mixed = total(mixed_kept, mixed_got)
    grad_in = total(kept, swap(sent))
    out_shape = tokens.shape[:3] + (width,)
    return (mixed.reshape(out_shape), grad_in.reshape(out_shape))


def solution(mesh):
    placed = (
        P("height", "width", None, None),
        P("height", "width", None, None),
        P(("height", "width"), None, "head"),
        P(("height", "width"), "head"),
        P("head"),
        P("head"),
        P("height", "width", None),
    )
    return jax.shard_map(
        on_device,
        mesh=mesh,
        in_specs=placed,
        out_specs=(P("height", "width", None, "head"), P("height", "width", None, "head")),
        check_vma=False,
    )
```

```python
import functools

import jax
import jax.numpy as jnp
from jax import lax
from jax.experimental import pallas as pl
from jax.experimental.pallas import tpu as pltpu
from jax.sharding import PartitionSpec as P

HEAD_DIM = 128
LANES = 128
TILE = 144
COLUMN = 3 * TILE
WINDOW = 9 * TILE
EXTENDED = 12 * TILE
OWN_TILES = (4, 7)
MASK_LANE = 18
MASK_DEPTH = 1e5
FACTOR = HEAD_DIM ** (-0.5)
VMEM_BYTES = 50 * 1024 * 1024
epsilon = 1e-06


def dot_rows(left, right):
    return lax.dot_general(left, right, (((1,), (1,)), ((), ())), preferred_element_type=jnp.float32)


def dot_plain(left, right):
    return jnp.dot(left, right, preferred_element_type=jnp.float32)


def lane_index(rows):
    return lax.broadcasted_iota(jnp.int32, (rows, LANES), 1)


def norm_inverse(raw_values):
    return lax.rsqrt(jnp.mean(raw_values * raw_values, axis=-1, keepdims=True) + epsilon)


def norm_backward(raw_values, gain_vec, upstream):
    inverse = norm_inverse(raw_values)
    weighted = gain_vec * upstream
    inner_mean = jnp.mean(weighted * raw_values, axis=-1, keepdims=True)
    return inverse * weighted - raw_values * (inverse * inverse * inverse) * inner_mean


def three_parts(values):
    first = values.astype(jnp.bfloat16)
    rest = values - first.astype(jnp.float32)
    second = rest.astype(jnp.bfloat16)
    third = (rest - second.astype(jnp.float32)).astype(jnp.bfloat16)
    return [part.astype(jnp.float32) for part in (first, second, third)]


def extended_copies(own, up, down, left, right, target, sems):
    tile = lambda ref, i: ref.at[pl.ds(i * TILE, TILE)]
    pairs = [
        (left, 0, 3),
        (tile(up, 0), 3, 1),
        (tile(own, 0), 4, 1),
        (tile(down, 0), 5, 1),
        (tile(up, 1), 6, 1),
        (tile(own, 1), 7, 1),
        (tile(down, 1), 8, 1),
        (right, 9, 3),
    ]
    return [
        pltpu.make_async_copy(src, target.at[pl.ds(at * TILE, count * TILE)], sems.at[n])
        for n, (src, at, count) in enumerate(pairs)
    ]


def front_kernel(place, own, up, down, left, right, upstream, *rest):
    pieces, rest = rest[:4], rest[4:]
    (q_gain, k_gain, whole_out, own_keys, own_values, own_marks, own_k_raw, grad_q, attended, message,
     whole, tok, grad, keys, values, marks, own_raw, own_queries, token_sems, block_sems, grad_sem, whole_sem) = rest
    here = place[0]
    north, south = lax.rem(here + 12, 16), lax.rem(here + 4, 16)
    far = lax.rem(here + 8, 16)
    near = [here, here ^ 2, north, north ^ 2, south, south ^ 2]
    spots = [near, [far, far ^ 2], [spot ^ 1 for spot in near], [far ^ 1, far ^ 3]]
    parts = [(piece, n, spot) for piece, some in zip(pieces, spots) for n, spot in enumerate(some)]
    block_copies = [
        pltpu.make_async_copy(
            piece.at[pl.ds(n * 96, 96)], whole.at[pl.ds(pl.multiple_of(spot * 96, 96), 96)], block_sems.at[i]
        )
        for i, (piece, n, spot) in enumerate(parts)
    ]
    grad_copy = pltpu.make_async_copy(upstream, grad, grad_sem.at[0])
    token_copies = extended_copies(own, up, down, left, right, tok, token_sems)
    whole_copy = pltpu.make_async_copy(whole, whole_out, whole_sem.at[0])
    for copy in block_copies + [grad_copy] + token_copies:
        copy.start()
    for copy in block_copies + [grad_copy]:
        copy.wait()
    whole_copy.start()
    inner = own_keys.shape[1]
    heads = range(inner // HEAD_DIM)
    model = whole.shape[0]
    message[:, :inner] = dot_plain(grad[...], whole[:, 3 * inner :]).astype(jnp.bfloat16)
    for copy in token_copies:
        copy.wait()
    chunk = 2 * TILE

    for tile, at in enumerate(OWN_TILES):
        mine = slice(tile * TILE, (tile + 1) * TILE)
        own_queries[mine, :] = tok[at * TILE : (at + 1) * TILE, :model]
    result = dot_plain(own_queries[:, :model], whole[:, :inner])
    own_raw[...] = result
    for head in heads:
        lanes = slice(head * HEAD_DIM, (head + 1) * HEAD_DIM)
        own_queries[:, lanes] = (result[:, lanes] * norm_inverse(result[:, lanes]) * q_gain[:, lanes]).astype(jnp.bfloat16)

    def project(step, carry):
        rows = pl.ds(pl.multiple_of(step * chunk, chunk), chunk)
        result = dot_plain(tok[rows, :model], whole[:, inner : 3 * inner])
        for head in heads:
            lanes = slice(head * HEAD_DIM, (head + 1) * HEAD_DIM)
            k_raw = result[:, lanes]
            keys[rows, lanes] = (k_raw * norm_inverse(k_raw) * k_gain[:, lanes]).astype(jnp.bfloat16)
        values[rows, :] = result[:, inner:].astype(jnp.bfloat16)
        valid = tok[rows, model:].astype(jnp.float32)
        deep = jnp.where(lane_index(chunk) == MASK_LANE, MASK_DEPTH, 0.0)
        marks[rows, :] = (valid * deep - deep).astype(jnp.bfloat16)
        for tile, at in enumerate(OWN_TILES):
            offset = at * TILE % chunk

            @pl.when(step == at * TILE // chunk)
            def keep():
                own_k_raw[tile * TILE : (tile + 1) * TILE, :] = result[offset : offset + TILE, :inner]

        return carry

    lax.fori_loop(0, EXTENDED // chunk, project, 0, unroll=True)
    lane = lane_index(TILE)
    one_mark = jnp.where(lane == MASK_LANE, 1.0, 0.0)
    for tile, at in enumerate(OWN_TILES):
        mine = slice(tile * TILE, (tile + 1) * TILE)
        ext = slice(at * TILE, (at + 1) * TILE)
        window = slice(tile * COLUMN, tile * COLUMN + WINDOW)
        stats = one_mark
        for head in heads:
            lanes = slice(head * HEAD_DIM, (head + 1) * HEAD_DIM)
            q_aug = jnp.concatenate([own_queries[mine, lanes], one_mark.astype(jnp.bfloat16)], axis=1)
            win_keys = keys[window, lanes]
            win_values = values[window, lanes]
            k_aug = jnp.concatenate([win_keys, marks[window, :]], axis=1)
            weights = jnp.exp(dot_rows(q_aug, k_aug) * FACTOR)
            total = jnp.sum(weights, axis=-1, keepdims=True)
            probs = weights * (1.0 / total)
            attended[mine, lanes] = dot_plain(probs.astype(jnp.bfloat16), win_values).astype(jnp.bfloat16)
            grad_probs = dot_rows(message[mine, lanes], win_values)
            delta = jnp.sum(probs * grad_probs, axis=-1, keepdims=True)
            grad_scores = (probs * (grad_probs - delta)).astype(jnp.bfloat16)
            upstream_q = dot_plain(grad_scores, win_keys) * FACTOR
            grad_q[mine, lanes] = norm_backward(own_raw[mine, lanes], q_gain[:, lanes], upstream_q).astype(jnp.bfloat16)
            for n, part in enumerate(three_parts(jnp.log(total) * (1.0 / FACTOR))):
                stats = jnp.where(lane == 3 * head + n, part, stats)
            for n, part in enumerate(three_parts(delta)):
                stats = jnp.where(lane == 9 + 3 * head + n, part, stats)
        message[mine, inner:] = stats.astype(jnp.bfloat16)
        own_keys[mine, :] = keys[ext, :]
        own_values[mine, :] = values[ext, :]
        own_marks[mine, :] = marks[ext, :]
    whole_copy.wait()


def queries_kernel(own, up, down, left, right, whole, q_gain, queries, weight, tok, sems, weight_sem):
    inner = weight.shape[1]
    model = weight.shape[0]
    weight_copy = pltpu.make_async_copy(whole.at[:, pl.ds(0, inner)], weight, weight_sem.at[0])
    copies = extended_copies(own, up, down, left, right, tok, sems)
    for copy in [weight_copy] + copies:
        copy.start()
    for copy in [weight_copy] + copies:
        copy.wait()
    chunk = 4 * TILE

    def project(step, carry):
        rows = pl.ds(pl.multiple_of(step * chunk, chunk), chunk)
        result = dot_plain(tok[rows, :model], weight[...])
        for head in range(inner // HEAD_DIM):
            lanes = slice(head * HEAD_DIM, (head + 1) * HEAD_DIM)
            q_raw = result[:, lanes]
            queries[rows, lanes] = (q_raw * norm_inverse(q_raw) * q_gain[:, lanes]).astype(jnp.bfloat16)
        return carry

    lax.fori_loop(0, EXTENDED // chunk, project, 0)


def back_kernel(place, own, up, down, left, right, queries, keys, values, marks, k_raw, grad_q, whole, k_gain,
                kept, sent, ext, grad_qkv, weight, sems, weight_sem):
    inner = queries.shape[1]
    copies = extended_copies(own, up, down, left, right, ext, sems)
    weight_copy = pltpu.make_async_copy(whole.at[:, pl.ds(0, 3 * inner)], weight, weight_sem.at[0])
    for copy in copies + [weight_copy]:
        copy.start()
    for copy in copies:
        copy.wait()
    grad_qkv[:, :inner] = grad_q[...]
    lane = lane_index(TILE)
    for tile in range(2):
        mine = slice(tile * TILE, (tile + 1) * TILE)
        window = slice(tile * COLUMN, tile * COLUMN + WINDOW)
        stats = ext[window, inner:]
        for head in range(inner // HEAD_DIM):
            lanes = slice(head * HEAD_DIM, (head + 1) * HEAD_DIM)
            k_signs = jnp.where((lane >= 3 * head) & (lane < 3 * head + 3), -1.0, 0.0).astype(jnp.bfloat16)
            v_signs = jnp.where((lane >= 9 + 3 * head) & (lane < 12 + 3 * head), -1.0, 0.0).astype(jnp.bfloat16)
            k_aug = jnp.concatenate([keys[mine, lanes], marks[mine, :] + k_signs], axis=1)
            v_aug = jnp.concatenate([values[mine, lanes], v_signs], axis=1)
            win_queries = queries[window, lanes]
            win_upstream = ext[window, lanes]
            probs = jnp.exp(dot_rows(k_aug, jnp.concatenate([win_queries, stats], axis=1)) * FACTOR)
            centred = dot_rows(v_aug, jnp.concatenate([win_upstream, stats], axis=1))
            grad_scores = (probs * centred).astype(jnp.bfloat16)
            grad_v = dot_plain(probs.astype(jnp.bfloat16), win_upstream)
            upstream_k = dot_plain(grad_scores, win_queries) * FACTOR
            grad_k = norm_backward(k_raw[mine, lanes], k_gain[:, lanes], upstream_k)
            grad_qkv[mine, inner + head * HEAD_DIM : inner + (head + 1) * HEAD_DIM] = grad_k.astype(jnp.bfloat16)
            grad_qkv[mine, 2 * inner + head * HEAD_DIM : 2 * inner + (head + 1) * HEAD_DIM] = grad_v.astype(jnp.bfloat16)
    weight_copy.wait()
    half = kept.shape[1]
    for target, group in ((sent, 1 - place[1]), (kept, place[1])):
        rows = pl.ds(pl.multiple_of(group * half, half), half)
        target[...] = dot_rows(grad_qkv[...], weight[rows, :]).astype(jnp.bfloat16)


def steps(axis, shift, wrap=False):
    count = lax.axis_size(axis)
    return [(i, (i + shift) % count) for i in range(count) if wrap or 0 <= i + shift < count]


def spread_height(own):
    up = lax.ppermute(own, "height", steps("height", 1))
    down = lax.ppermute(own, "height", steps("height", -1))
    return up, down


def spread_width(first, last):
    left = lax.ppermute(last, "width", steps("width", 1))
    right = lax.ppermute(first, "width", steps("width", -1))
    return left, right


def joined_columns(up, own, down):
    return [jnp.concatenate([part[i * TILE : (i + 1) * TILE] for part in (up, own, down)], axis=0) for i in (0, 1)]


def flip(x, bit):
    count = lax.axis_size("height")
    return lax.ppermute(x, "height", [(i, i ^ bit) for i in range(count)])


def gather_height(block, up, own, down):
    shift = lambda x, by: lax.ppermute(x, "height", steps("height", by, True))
    rows = block.shape[0]
    pair = jnp.concatenate([block, flip(block, 2)], axis=0)
    pair, first, last = lax.optimization_barrier((pair, *columns(up, own, down)))
    left, right = spread_width(first, last)
    north, south = shift(pair, 4), shift(pair, -4)
    far, far_beside = shift(north[:rows], 4), shift(south[rows:], -4)
    near = jnp.concatenate([pair, north, south], axis=0)
    near, far = lax.optimization_barrier((near, far))
    near_swapped = flip(near, 1)
    far_beside, left, right = lax.optimization_barrier((far_beside, left, right))
    far = jnp.concatenate([far, far_beside], axis=0)
    return [near, far, near_swapped, flip(far, 1)], left, right


def columns_kernel(up, own, down, first, last, sems):
    copies = [
        pltpu.make_async_copy(part.at[pl.ds(side * TILE, TILE)], target.at[pl.ds(n * TILE, TILE)], sems.at[3 * side + n])
        for side, target in enumerate((first, last))
        for n, part in enumerate((up, own, down))
    ]
    for copy in copies:
        copy.start()
    for copy in copies:
        copy.wait()


def columns(up, own, down):
    anywhere = pl.BlockSpec(memory_space=pl.ANY)
    out = jax.ShapeDtypeStruct((COLUMN, own.shape[1]), own.dtype)
    return pl.pallas_call(
        columns_kernel,
        out_shape=(out, out),
        in_specs=[anywhere] * 3,
        out_specs=(whole_spec(), whole_spec()),
        scratch_shapes=[pltpu.SemaphoreType.DMA((6,))],
        compiler_params=pltpu.CompilerParams(vmem_limit_bytes=VMEM_BYTES),
        name="columns",
    )(up, own, down)


def whole_spec():
    return pl.BlockSpec(memory_space=pltpu.VMEM)


def on_device(tokens, grad_out, qkv_weight, out_weight, q_gain, k_gain, key_valid):
    model = tokens.shape[-1]
    inner = q_gain.shape[0]
    count = tokens.shape[0] * tokens.shape[1] * tokens.shape[2]
    shard_rows = qkv_weight.shape[0]
    place = jnp.stack([lax.axis_index("height"), lax.axis_index("head")]).astype(jnp.int32)
    valid = key_valid.reshape(count, 1).astype(jnp.bfloat16)
    marked = jnp.concatenate([tokens.reshape(count, model), jnp.broadcast_to(valid, (count, LANES))], axis=1)
    up, down = spread_height(marked)
    joined = jnp.concatenate([qkv_weight.reshape(shard_rows, 3 * inner), out_weight], axis=1)
    along_width = lax.all_gather(joined, "width", axis=0, tiled=True)
    along_width, up, down = lax.optimization_barrier((along_width, up, down))
    blocks, left, right = gather_height(along_width, up, marked, down)
    q_gains, k_gains = q_gain.reshape(1, inner), k_gain.reshape(1, inner)
    anywhere = pl.BlockSpec(memory_space=pl.ANY)
    shape = jax.ShapeDtypeStruct
    half = jnp.bfloat16
    whole, keys, values, marks, k_raw, grad_q, attended, message = pl.pallas_call(
        front_kernel,
        out_shape=(
            shape((model, 4 * inner), half),
            shape((count, inner), half),
            shape((count, inner), half),
            shape((count, LANES), half),
            shape((count, inner), jnp.float32),
            shape((count, inner), half),
            shape((count, inner), half),
            shape((count, inner + LANES), half),
        ),
        in_specs=[pl.BlockSpec(memory_space=pltpu.SMEM)] + [anywhere] * 10 + [whole_spec()] * 2,
        out_specs=(anywhere,) + tuple(whole_spec() for _ in range(7)),
        scratch_shapes=[
            pltpu.VMEM((model, 4 * inner), half),
            pltpu.VMEM((EXTENDED, model + LANES), half),
            pltpu.VMEM((count, model), half),
            pltpu.VMEM((EXTENDED, inner), half),
            pltpu.VMEM((EXTENDED, inner), half),
            pltpu.VMEM((EXTENDED, LANES), half),
            pltpu.VMEM((count, inner), jnp.float32),
            pltpu.VMEM((count, model), half),
            pltpu.SemaphoreType.DMA((8,)),
            pltpu.SemaphoreType.DMA((16,)),
            pltpu.SemaphoreType.DMA((1,)),
            pltpu.SemaphoreType.DMA((1,)),
        ],
        compiler_params=pltpu.CompilerParams(vmem_limit_bytes=VMEM_BYTES),
        name="front",
    )(place, marked, up, down, left, right, grad_out.reshape(count, model), *blocks, q_gains, k_gains)

    group = lax.axis_index("head")
    width = model // 2
    swap = lambda x: lax.ppermute(x, "head", [(0, 1), (1, 0)])
    part = lambda which: lax.dynamic_slice(whole, (which * width, 3 * inner), (width, inner))
    beyond = (marked, up, down, left, right)
    up, down = spread_height(message)
    mixed_sent = dot_rows(attended, part(1 - group)).astype(half)
    up, down, mixed_sent = lax.optimization_barrier((up, down, mixed_sent))
    mixed_kept = dot_rows(attended, part(group)).astype(half)
    mixed_got = swap(mixed_sent)
    left, right = spread_width(*joined_columns(up, message, down))
    up, *beyond = lax.optimization_barrier((up, *beyond))
    queries = pl.pallas_call(
        queries_kernel,
        out_shape=shape((EXTENDED, inner), half),
        in_specs=[anywhere] * 6 + [whole_spec()],
        out_specs=whole_spec(),
        scratch_shapes=[
            pltpu.VMEM((model, inner), half),
            pltpu.VMEM((EXTENDED, model + LANES), half),
            pltpu.SemaphoreType.DMA((8,)),
            pltpu.SemaphoreType.DMA((1,)),
        ],
        compiler_params=pltpu.CompilerParams(vmem_limit_bytes=VMEM_BYTES),
        cost_estimate=pl.CostEstimate(flops=2 * EXTENDED * model * inner, bytes_accessed=8 * 2**20, transcendentals=0),
        name="queries",
    )(*beyond, whole, q_gains)
    kept, sent = pl.pallas_call(
        back_kernel,
        out_shape=(shape((count, width), half), shape((count, width), half)),
        in_specs=[pl.BlockSpec(memory_space=pltpu.SMEM)] + [anywhere] * 5 + [whole_spec()] * 6 + [anywhere, whole_spec()],
        out_specs=(whole_spec(), whole_spec()),
        scratch_shapes=[
            pltpu.VMEM((EXTENDED, inner + LANES), half),
            pltpu.VMEM((count, 3 * inner), half),
            pltpu.VMEM((model, 3 * inner), half),
            pltpu.SemaphoreType.DMA((8,)),
            pltpu.SemaphoreType.DMA((1,)),
        ],
        compiler_params=pltpu.CompilerParams(vmem_limit_bytes=VMEM_BYTES),
        name="back",
    )(place, message, up, down, left, right, queries, keys, values, marks, k_raw, grad_q, whole, k_gains)
    total = lambda a, b: (a.astype(jnp.float32) + b.astype(jnp.float32)).astype(half)
    mixed = total(mixed_kept, mixed_got)
    grad_in = total(kept, swap(sent))
    out_shape = tokens.shape[:3] + (width,)
    return (mixed.reshape(out_shape), grad_in.reshape(out_shape))


def solution(mesh):
    placed = (
        P("height", "width", None, None),
        P("height", "width", None, None),
        P(("height", "width"), None, "head"),
        P(("height", "width"), "head"),
        P("head"),
        P("head"),
        P("height", "width", None),
    )
    return jax.shard_map(
        on_device,
        mesh=mesh,
        in_specs=placed,
        out_specs=(P("height", "width", None, "head"), P("height", "width", None, "head")),
        check_vma=False,
    )
```

```python
import functools

import jax
import jax.numpy as jnp
from jax import lax
from jax.experimental import pallas as pl
from jax.experimental.pallas import tpu as pltpu
from jax.sharding import PartitionSpec as P

HEAD_DIM = 128
LANES = 128
TILE = 144
COLUMN = 3 * TILE
WINDOW = 9 * TILE
EXTENDED = 12 * TILE
OWN_TILES = (4, 7)
MASK_LANE = 18
MASK_DEPTH = 1e5
FACTOR = HEAD_DIM ** (-0.5)
VMEM_BYTES = 50 * 1024 * 1024
epsilon = 1e-06


def dot_rows(left, right):
    return lax.dot_general(left, right, (((1,), (1,)), ((), ())), preferred_element_type=jnp.float32)


def dot_plain(left, right):
    return jnp.dot(left, right, preferred_element_type=jnp.float32)


def lane_index(rows):
    return lax.broadcasted_iota(jnp.int32, (rows, LANES), 1)


def norm_inverse(raw_values):
    return lax.rsqrt(jnp.mean(raw_values * raw_values, axis=-1, keepdims=True) + epsilon)


def norm_backward(raw_values, gain_vec, upstream):
    inverse = norm_inverse(raw_values)
    weighted = gain_vec * upstream
    inner_mean = jnp.mean(weighted * raw_values, axis=-1, keepdims=True)
    return inverse * weighted - raw_values * (inverse * inverse * inverse) * inner_mean


def three_parts(values):
    first = values.astype(jnp.bfloat16)
    rest = values - first.astype(jnp.float32)
    second = rest.astype(jnp.bfloat16)
    third = (rest - second.astype(jnp.float32)).astype(jnp.bfloat16)
    return [part.astype(jnp.float32) for part in (first, second, third)]


def extended_copies(own, up, down, left, right, target, sems):
    tile = lambda ref, i: ref.at[pl.ds(i * TILE, TILE)]
    pairs = [
        (left, 0, 3),
        (tile(up, 0), 3, 1),
        (tile(own, 0), 4, 1),
        (tile(down, 0), 5, 1),
        (tile(up, 1), 6, 1),
        (tile(own, 1), 7, 1),
        (tile(down, 1), 8, 1),
        (right, 9, 3),
    ]
    return [
        pltpu.make_async_copy(src, target.at[pl.ds(at * TILE, count * TILE)], sems.at[n])
        for n, (src, at, count) in enumerate(pairs)
    ]


def token_copies_of(core, own, up, down, left, right, shared, target, sems):
    pairs = [
        (left, 0, 2, core),
        (shared, 0, 1, 2 - 2 * core),
        (up, 0, 1, 3),
        (own, 0, 1, 4),
        (down, 0, 1, 5),
        (up, 1, 1, 6),
        (own, 1, 1, 7),
        (down, 1, 1, 8),
        (right, 0, 2, 9 + core),
        (shared, 1, 1, 11 - 2 * core),
    ]
    return [
        pltpu.make_async_copy(
            src.at[pl.ds(first * TILE, count * TILE)],
            target.at[pl.ds(pl.multiple_of(at * TILE, TILE), count * TILE)],
            sems.at[n],
        )
        for n, (src, first, count, at) in enumerate(pairs)
    ]


def front_kernel(place, own, up, down, left, right, shared, upstream, *rest):
    pieces, rest = rest[:4], rest[4:]
    (q_gain, k_gain, whole_out, own_keys, own_values, own_marks, own_k_raw, grad_q, attended, message,
     whole, tok, grad, keys, values, marks, own_raw, own_queries, token_sems, block_sems, grad_sem, whole_sem) = rest
    here = place[0]
    north, south = lax.rem(here + 12, 16), lax.rem(here + 4, 16)
    far = lax.rem(here + 8, 16)
    near = [here, here ^ 2, north, north ^ 2, south, south ^ 2]
    spots = [near, [far, far ^ 2], [spot ^ 1 for spot in near], [far ^ 1, far ^ 3]]
    parts = [(piece, n, spot) for piece, some in zip(pieces, spots) for n, spot in enumerate(some)]
    block_copies = [
        pltpu.make_async_copy(
            piece.at[pl.ds(n * 96, 96)], whole.at[pl.ds(pl.multiple_of(spot * 96, 96), 96)], block_sems.at[i]
        )
        for i, (piece, n, spot) in enumerate(parts)
    ]
    grad_copy = pltpu.make_async_copy(upstream, grad, grad_sem.at[0])
    token_copies = token_copies_of(lax.rem(here, 2), own, up, down, left, right, shared, tok, token_sems)
    whole_copy = pltpu.make_async_copy(whole, whole_out, whole_sem.at[0])
    for copy in block_copies + [grad_copy] + token_copies:
        copy.start()
    for copy in block_copies + [grad_copy]:
        copy.wait()
    whole_copy.start()
    inner = own_keys.shape[1]
    heads = range(inner // HEAD_DIM)
    model = whole.shape[0]
    message[:, :inner] = dot_plain(grad[...], whole[:, 3 * inner :]).astype(jnp.bfloat16)
    for copy in token_copies:
        copy.wait()
    chunk = 2 * TILE

    for tile, at in enumerate(OWN_TILES):
        mine = slice(tile * TILE, (tile + 1) * TILE)
        own_queries[mine, :] = tok[at * TILE : (at + 1) * TILE, :model]
    result = dot_plain(own_queries[:, :model], whole[:, :inner])
    own_raw[...] = result
    for head in heads:
        lanes = slice(head * HEAD_DIM, (head + 1) * HEAD_DIM)
        own_queries[:, lanes] = (result[:, lanes] * norm_inverse(result[:, lanes]) * q_gain[:, lanes]).astype(jnp.bfloat16)

    def project(step, carry):
        rows = pl.ds(pl.multiple_of(step * chunk, chunk), chunk)
        result = dot_plain(tok[rows, :model], whole[:, inner : 3 * inner])
        for head in heads:
            lanes = slice(head * HEAD_DIM, (head + 1) * HEAD_DIM)
            k_raw = result[:, lanes]
            keys[rows, lanes] = (k_raw * norm_inverse(k_raw) * k_gain[:, lanes]).astype(jnp.bfloat16)
        values[rows, :] = result[:, inner:].astype(jnp.bfloat16)
        valid = tok[rows, model:].astype(jnp.float32)
        deep = jnp.where(lane_index(chunk) == MASK_LANE, MASK_DEPTH, 0.0)
        marks[rows, :] = (valid * deep - deep).astype(jnp.bfloat16)
        for tile, at in enumerate(OWN_TILES):
            offset = at * TILE % chunk

            @pl.when(step == at * TILE // chunk)
            def keep():
                own_k_raw[tile * TILE : (tile + 1) * TILE, :] = result[offset : offset + TILE, :inner]

        return carry

    lax.fori_loop(0, EXTENDED // chunk, project, 0, unroll=True)
    lane = lane_index(TILE)
    one_mark = jnp.where(lane == MASK_LANE, 1.0, 0.0)
    for tile, at in enumerate(OWN_TILES):
        mine = slice(tile * TILE, (tile + 1) * TILE)
        ext = slice(at * TILE, (at + 1) * TILE)
        window = slice(tile * COLUMN, tile * COLUMN + WINDOW)
        stats = one_mark
        for head in heads:
            lanes = slice(head * HEAD_DIM, (head + 1) * HEAD_DIM)
            q_aug = jnp.concatenate([own_queries[mine, lanes], one_mark.astype(jnp.bfloat16)], axis=1)
            win_keys = keys[window, lanes]
            win_values = values[window, lanes]
            k_aug = jnp.concatenate([win_keys, marks[window, :]], axis=1)
            weights = jnp.exp(dot_rows(q_aug, k_aug) * FACTOR)
            total = jnp.sum(weights, axis=-1, keepdims=True)
            probs = weights * (1.0 / total)
            attended[mine, lanes] = dot_plain(probs.astype(jnp.bfloat16), win_values).astype(jnp.bfloat16)
            grad_probs = dot_rows(message[mine, lanes], win_values)
            delta = jnp.sum(probs * grad_probs, axis=-1, keepdims=True)
            grad_scores = (probs * (grad_probs - delta)).astype(jnp.bfloat16)
            upstream_q = dot_plain(grad_scores, win_keys) * FACTOR
            grad_q[mine, lanes] = norm_backward(own_raw[mine, lanes], q_gain[:, lanes], upstream_q).astype(jnp.bfloat16)
            for n, part in enumerate(three_parts(jnp.log(total) * (1.0 / FACTOR))):
                stats = jnp.where(lane == 3 * head + n, part, stats)
            for n, part in enumerate(three_parts(delta)):
                stats = jnp.where(lane == 9 + 3 * head + n, part, stats)
        message[mine, inner:] = stats.astype(jnp.bfloat16)
        own_keys[mine, :] = keys[ext, :]
        own_values[mine, :] = values[ext, :]
        own_marks[mine, :] = marks[ext, :]
    whole_copy.wait()


def queries_kernel(place, own, up, down, left, right, shared, whole, q_gain, queries, weight, tok, sems, weight_sem):
    inner = weight.shape[1]
    model = weight.shape[0]
    weight_copy = pltpu.make_async_copy(whole.at[:, pl.ds(0, inner)], weight, weight_sem.at[0])
    copies = token_copies_of(lax.rem(place[0], 2), own, up, down, left, right, shared, tok, sems)
    for copy in [weight_copy] + copies:
        copy.start()
    for copy in [weight_copy] + copies:
        copy.wait()
    chunk = 4 * TILE

    def project(step, carry):
        rows = pl.ds(pl.multiple_of(step * chunk, chunk), chunk)
        result = dot_plain(tok[rows, :model], weight[...])
        for head in range(inner // HEAD_DIM):
            lanes = slice(head * HEAD_DIM, (head + 1) * HEAD_DIM)
            q_raw = result[:, lanes]
            queries[rows, lanes] = (q_raw * norm_inverse(q_raw) * q_gain[:, lanes]).astype(jnp.bfloat16)
        return carry

    lax.fori_loop(0, EXTENDED // chunk, project, 0, unroll=True)


def back_kernel(place, own, up, down, left, right, queries_in, keys_in, values_in, marks_in, k_raw_in, grad_q_in, whole,
                k_gain, kept, sent, ext, grad_qkv, weight, queries, keys, values, marks, k_raw, sems, load_sems, weight_sem):
    inner = queries.shape[1]
    loads = [
        pltpu.make_async_copy(src, dst, load_sems.at[n])
        for n, (src, dst) in enumerate((
            (queries_in, queries),
            (keys_in, keys),
            (values_in, values),
            (marks_in, marks),
            (k_raw_in, k_raw),
            (grad_q_in, grad_qkv.at[:, pl.ds(0, inner)]),
        ))
    ]
    copies = extended_copies(own, up, down, left, right, ext, sems)
    weight_copy = pltpu.make_async_copy(whole.at[:, pl.ds(0, 3 * inner)], weight, weight_sem.at[0])
    for copy in copies + loads + [weight_copy]:
        copy.start()
    for copy in copies + loads:
        copy.wait()
    lane = lane_index(TILE)
    for tile in range(2):
        mine = slice(tile * TILE, (tile + 1) * TILE)
        window = slice(tile * COLUMN, tile * COLUMN + WINDOW)
        stats = ext[window, inner:]
        for head in range(inner // HEAD_DIM):
            lanes = slice(head * HEAD_DIM, (head + 1) * HEAD_DIM)
            k_signs = jnp.where((lane >= 3 * head) & (lane < 3 * head + 3), -1.0, 0.0).astype(jnp.bfloat16)
            v_signs = jnp.where((lane >= 9 + 3 * head) & (lane < 12 + 3 * head), -1.0, 0.0).astype(jnp.bfloat16)
            k_aug = jnp.concatenate([keys[mine, lanes], marks[mine, :] + k_signs], axis=1)
            v_aug = jnp.concatenate([values[mine, lanes], v_signs], axis=1)
            win_queries = queries[window, lanes]
            win_upstream = ext[window, lanes]
            probs = jnp.exp(dot_rows(k_aug, jnp.concatenate([win_queries, stats], axis=1)) * FACTOR)
            centred = dot_rows(v_aug, jnp.concatenate([win_upstream, stats], axis=1))
            grad_scores = (probs * centred).astype(jnp.bfloat16)
            grad_v = dot_plain(probs.astype(jnp.bfloat16), win_upstream)
            upstream_k = dot_plain(grad_scores, win_queries) * FACTOR
            grad_k = norm_backward(k_raw[mine, lanes], k_gain[:, lanes], upstream_k)
            grad_qkv[mine, inner + head * HEAD_DIM : inner + (head + 1) * HEAD_DIM] = grad_k.astype(jnp.bfloat16)
            grad_qkv[mine, 2 * inner + head * HEAD_DIM : 2 * inner + (head + 1) * HEAD_DIM] = grad_v.astype(jnp.bfloat16)
    weight_copy.wait()
    half = kept.shape[1]
    for target, group in ((sent, 1 - place[1]), (kept, place[1])):
        rows = pl.ds(pl.multiple_of(group * half, half), half)
        target[...] = dot_rows(grad_qkv[...], weight[rows, :]).astype(jnp.bfloat16)


def steps(axis, shift, wrap=False):
    count = lax.axis_size(axis)
    return [(i, (i + shift) % count) for i in range(count) if wrap or 0 <= i + shift < count]


def spread_height(own):
    up = lax.ppermute(own, "height", steps("height", 1))
    down = lax.ppermute(own, "height", steps("height", -1))
    return up, down


def spread_width(first, last):
    left = lax.ppermute(last, "width", steps("width", 1))
    right = lax.ppermute(first, "width", steps("width", -1))
    return left, right


def joined_columns(up, own, down):
    return [jnp.concatenate([part[i * TILE : (i + 1) * TILE] for part in (up, own, down)], axis=0) for i in (0, 1)]


def flip(x, bit):
    count = lax.axis_size("height")
    return lax.ppermute(x, "height", [(i, i ^ bit) for i in range(count)])


def gather_height(block, place, up, own, down):
    shift = lambda x, by: lax.ppermute(x, "height", steps("height", by, True))
    rows = block.shape[0]
    pair = jnp.concatenate([block, flip(block, 2)], axis=0)
    pair, first, last = lax.optimization_barrier((pair, *columns(place, up, own, down)))
    left, right = spread_width(first, last)
    core = place[0] & 1
    give = lambda part: lax.dynamic_slice(part, ((1 - core) * TILE, 0), (TILE, part.shape[1]))
    shared = flip(jnp.concatenate([give(left), give(right)], axis=0), 1)
    north, south = shift(pair, 4), shift(pair, -4)
    far, far_beside = shift(north[:rows], 4), shift(south[rows:], -4)
    near = jnp.concatenate([pair, north, south], axis=0)
    near, far = lax.optimization_barrier((near, far))
    far = jnp.concatenate([far, far_beside], axis=0)
    return [near, far, flip(near, 1), flip(far, 1)], left, right, shared


def columns_kernel(place, up, own, down, first, last, sems):
    def copy_all(upper, lower):
        copies = [
            pltpu.make_async_copy(part.at[pl.ds(side * TILE, TILE)], target.at[pl.ds(n * TILE, TILE)], sems.at[2 * side + n])
            for side, target in enumerate((first, last))
            for n, part in enumerate((upper, lower))
        ]
        for copy in copies:
            copy.start()
        for copy in copies:
            copy.wait()

    @pl.when(place[0] % 2 == 0)
    def even():
        copy_all(up, own)

    @pl.when(place[0] % 2 == 1)
    def odd():
        copy_all(own, down)


def columns(place, up, own, down):
    anywhere = pl.BlockSpec(memory_space=pl.ANY)
    out = jax.ShapeDtypeStruct((2 * TILE, own.shape[1]), own.dtype)
    return pl.pallas_call(
        columns_kernel,
        out_shape=(out, out),
        in_specs=[pl.BlockSpec(memory_space=pltpu.SMEM)] + [anywhere] * 3,
        out_specs=(whole_spec(), whole_spec()),
        scratch_shapes=[pltpu.SemaphoreType.DMA((4,))],
        compiler_params=pltpu.CompilerParams(vmem_limit_bytes=VMEM_BYTES),
        name="columns",
    )(place, up, own, down)


def whole_spec():
    return pl.BlockSpec(memory_space=pltpu.VMEM)


def on_device(tokens, grad_out, qkv_weight, out_weight, q_gain, k_gain, key_valid):
    model = tokens.shape[-1]
    inner = q_gain.shape[0]
    count = tokens.shape[0] * tokens.shape[1] * tokens.shape[2]
    shard_rows = qkv_weight.shape[0]
    place = jnp.stack([lax.axis_index("height"), lax.axis_index("head")]).astype(jnp.int32)
    valid = key_valid.reshape(count, 1).astype(jnp.bfloat16)
    marked = jnp.concatenate([tokens.reshape(count, model), jnp.broadcast_to(valid, (count, LANES))], axis=1)
    up, down = spread_height(marked)
    joined = jnp.concatenate([qkv_weight.reshape(shard_rows, 3 * inner), out_weight], axis=1)
    along_width = lax.all_gather(joined, "width", axis=0, tiled=True)
    along_width, up, down = lax.optimization_barrier((along_width, up, down))
    blocks, left, right, shared = gather_height(along_width, place, up, marked, down)
    q_gains, k_gains = q_gain.reshape(1, inner), k_gain.reshape(1, inner)
    anywhere = pl.BlockSpec(memory_space=pl.ANY)
    shape = jax.ShapeDtypeStruct
    half = jnp.bfloat16
    whole, keys, values, marks, k_raw, grad_q, attended, message = pl.pallas_call(
        front_kernel,
        out_shape=(
            shape((model, 4 * inner), half),
            shape((count, inner), half),
            shape((count, inner), half),
            shape((count, LANES), half),
            shape((count, inner), jnp.float32),
            shape((count, inner), half),
            shape((count, inner), half),
            shape((count, inner + LANES), half),
        ),
        in_specs=[pl.BlockSpec(memory_space=pltpu.SMEM)] + [anywhere] * 11 + [whole_spec()] * 2,
        out_specs=(anywhere,) + tuple(whole_spec() for _ in range(7)),
        scratch_shapes=[
            pltpu.VMEM((model, 4 * inner), half),
            pltpu.VMEM((EXTENDED, model + LANES), half),
            pltpu.VMEM((count, model), half),
            pltpu.VMEM((EXTENDED, inner), half),
            pltpu.VMEM((EXTENDED, inner), half),
            pltpu.VMEM((EXTENDED, LANES), half),
            pltpu.VMEM((count, inner), jnp.float32),
            pltpu.VMEM((count, model), half),
            pltpu.SemaphoreType.DMA((10,)),
            pltpu.SemaphoreType.DMA((16,)),
            pltpu.SemaphoreType.DMA((1,)),
            pltpu.SemaphoreType.DMA((1,)),
        ],
        compiler_params=pltpu.CompilerParams(vmem_limit_bytes=VMEM_BYTES),
        name="front",
    )(place, marked, up, down, left, right, shared, grad_out.reshape(count, model), *blocks, q_gains, k_gains)

    group = lax.axis_index("head")
    width = model // 2
    swap = lambda x: lax.ppermute(x, "head", [(0, 1), (1, 0)])
    part = lambda which: lax.dynamic_slice(whole, (which * width, 3 * inner), (width, inner))
    beyond = (marked, up, down, left, right, shared)
    up, down = spread_height(message)
    mixed_sent = dot_rows(attended, part(1 - group)).astype(half)
    up, down, mixed_sent = lax.optimization_barrier((up, down, mixed_sent))
    mixed_kept = dot_rows(attended, part(group)).astype(half)
    mixed_got = swap(mixed_sent)
    left, right = spread_width(*joined_columns(up, message, down))
    up, *beyond = lax.optimization_barrier((up, *beyond))
    queries = pl.pallas_call(
        queries_kernel,
        out_shape=shape((EXTENDED, inner), half),
        in_specs=[pl.BlockSpec(memory_space=pltpu.SMEM)] + [anywhere] * 7 + [whole_spec()],
        out_specs=whole_spec(),
        scratch_shapes=[
            pltpu.VMEM((model, inner), half),
            pltpu.VMEM((EXTENDED, model + LANES), half),
            pltpu.SemaphoreType.DMA((10,)),
            pltpu.SemaphoreType.DMA((1,)),
        ],
        compiler_params=pltpu.CompilerParams(vmem_limit_bytes=VMEM_BYTES),
        cost_estimate=pl.CostEstimate(flops=2 * EXTENDED * model * inner, bytes_accessed=8 * 2**20, transcendentals=0),
        name="queries",
    )(place, *beyond, whole, q_gains)
    kept, sent = pl.pallas_call(
        back_kernel,
        out_shape=(shape((count, width), half), shape((count, width), half)),
        in_specs=[pl.BlockSpec(memory_space=pltpu.SMEM)] + [anywhere] * 12 + [whole_spec()],
        out_specs=(whole_spec(), whole_spec()),
        scratch_shapes=[
            pltpu.VMEM((EXTENDED, inner + LANES), half),
            pltpu.VMEM((count, 3 * inner), half),
            pltpu.VMEM((model, 3 * inner), half),
            pltpu.VMEM((EXTENDED, inner), half),
            pltpu.VMEM((count, inner), half),
            pltpu.VMEM((count, inner), half),
            pltpu.VMEM((count, LANES), half),
            pltpu.VMEM((count, inner), jnp.float32),
            pltpu.SemaphoreType.DMA((8,)),
            pltpu.SemaphoreType.DMA((6,)),
            pltpu.SemaphoreType.DMA((1,)),
        ],
        compiler_params=pltpu.CompilerParams(vmem_limit_bytes=VMEM_BYTES),
        name="back",
    )(place, message, up, down, left, right, queries, keys, values, marks, k_raw, grad_q, whole, k_gains)
    total = lambda a, b: (a.astype(jnp.float32) + b.astype(jnp.float32)).astype(half)
    mixed = total(mixed_kept, mixed_got)
    grad_in = total(kept, swap(sent))
    out_shape = tokens.shape[:3] + (width,)
    return (mixed.reshape(out_shape), grad_in.reshape(out_shape))


def solution(mesh):
    placed = (
        P("height", "width", None, None),
        P("height", "width", None, None),
        P(("height", "width"), None, "head"),
        P(("height", "width"), "head"),
        P("head"),
        P("head"),
        P("height", "width", None),
    )
    return jax.shard_map(
        on_device,
        mesh=mesh,
        in_specs=placed,
        out_specs=(P("height", "width", None, "head"), P("height", "width", None, "head")),
        check_vma=False,
    )
```

```python
import functools

import jax
import jax.numpy as jnp
from jax import lax
from jax.experimental import pallas as pl
from jax.experimental.pallas import tpu as pltpu
from jax.sharding import PartitionSpec as P

HEAD_DIM = 128
LANES = 128
TILE = 144
COLUMN = 3 * TILE
WINDOW = 9 * TILE
EXTENDED = 12 * TILE
OWN_TILES = (4, 7)
MASK_LANE = 18
SIDE_LANES = (19, 20)
MASK_DEPTH = 1e5
FACTOR = HEAD_DIM ** (-0.5)
VMEM_BYTES = 50 * 1024 * 1024
epsilon = 1e-06


def dot_rows(left, right):
    return lax.dot_general(left, right, (((1,), (1,)), ((), ())), preferred_element_type=jnp.float32)


def dot_plain(left, right):
    return jnp.dot(left, right, preferred_element_type=jnp.float32)


def lane_index(rows):
    return lax.broadcasted_iota(jnp.int32, (rows, LANES), 1)


def side_rows(rows):
    row = lax.broadcasted_iota(jnp.int32, (rows, LANES), 0)
    lane = lane_index(rows)
    first = (row < TILE) & (lane == SIDE_LANES[0])
    second = (row >= TILE) & (lane == SIDE_LANES[1])
    return jnp.where(first | second, 1.0, 0.0)


def side_marks(start, rows):
    row = start + lax.broadcasted_iota(jnp.int32, (rows, LANES), 0)
    lane = lane_index(rows)
    last = (row >= WINDOW) & (lane == SIDE_LANES[0])
    first = (row < COLUMN) & (lane == SIDE_LANES[1])
    return jnp.where(first | last, -MASK_DEPTH, 0.0)


def norm_inverse(raw_values):
    return lax.rsqrt(jnp.mean(raw_values * raw_values, axis=-1, keepdims=True) + epsilon)


def norm_backward(raw_values, gain_vec, upstream):
    inverse = norm_inverse(raw_values)
    weighted = gain_vec * upstream
    inner_mean = jnp.mean(weighted * raw_values, axis=-1, keepdims=True)
    return inverse * weighted - raw_values * (inverse * inverse * inverse) * inner_mean


def three_parts(values):
    first = values.astype(jnp.bfloat16)
    rest = values - first.astype(jnp.float32)
    second = rest.astype(jnp.bfloat16)
    third = (rest - second.astype(jnp.float32)).astype(jnp.bfloat16)
    return [part.astype(jnp.float32) for part in (first, second, third)]


def extended_copies(own, up, down, left, right, target, sems):
    tile = lambda ref, i: ref.at[pl.ds(i * TILE, TILE)]
    pairs = [
        (left, 0, 3),
        (tile(up, 0), 3, 1),
        (tile(own, 0), 4, 1),
        (tile(down, 0), 5, 1),
        (tile(up, 1), 6, 1),
        (tile(own, 1), 7, 1),
        (tile(down, 1), 8, 1),
        (right, 9, 3),
    ]
    return [
        pltpu.make_async_copy(src, target.at[pl.ds(at * TILE, count * TILE)], sems.at[n])
        for n, (src, at, count) in enumerate(pairs)
    ]


def token_copies_of(core, own, up, down, left, right, shared, target, sems):
    pairs = [
        (left, 0, 2, core),
        (shared, 0, 1, 2 - 2 * core),
        (up, 0, 1, 3),
        (own, 0, 1, 4),
        (down, 0, 1, 5),
        (up, 1, 1, 6),
        (own, 1, 1, 7),
        (down, 1, 1, 8),
        (right, 0, 2, 9 + core),
        (shared, 1, 1, 11 - 2 * core),
    ]
    return [
        pltpu.make_async_copy(
            src.at[pl.ds(first * TILE, count * TILE)],
            target.at[pl.ds(pl.multiple_of(at * TILE, TILE), count * TILE)],
            sems.at[n],
        )
        for n, (src, first, count, at) in enumerate(pairs)
    ]


def front_kernel(place, own, up, down, left, right, shared, upstream, *rest):
    pieces, rest = rest[:4], rest[4:]
    (q_gain, k_gain, whole_out, own_keys, own_values, own_marks, own_k_raw, grad_q, attended, message,
     whole, tok, grad, keys, values, marks, own_raw, own_queries, token_sems, block_sems, grad_sem, whole_sem) = rest
    here = place[0]
    north, south = lax.rem(here + 12, 16), lax.rem(here + 4, 16)
    far = lax.rem(here + 8, 16)
    near = [here, here ^ 2, north, north ^ 2, south, south ^ 2]
    spots = [near, [far, far ^ 2], [spot ^ 1 for spot in near], [far ^ 1, far ^ 3]]
    parts = [(piece, n, spot) for piece, some in zip(pieces, spots) for n, spot in enumerate(some)]
    block_copies = [
        pltpu.make_async_copy(
            piece.at[pl.ds(n * 96, 96)], whole.at[pl.ds(pl.multiple_of(spot * 96, 96), 96)], block_sems.at[i]
        )
        for i, (piece, n, spot) in enumerate(parts)
    ]
    grad_copy = pltpu.make_async_copy(upstream, grad, grad_sem.at[0])
    token_copies = token_copies_of(lax.rem(here, 2), own, up, down, left, right, shared, tok, token_sems)
    whole_copy = pltpu.make_async_copy(whole, whole_out, whole_sem.at[0])
    for copy in block_copies + [grad_copy] + token_copies:
        copy.start()
    for copy in block_copies + [grad_copy]:
        copy.wait()
    whole_copy.start()
    inner = own_keys.shape[1]
    heads = range(inner // HEAD_DIM)
    model = whole.shape[0]
    message[:, :inner] = dot_plain(grad[...], whole[:, 3 * inner :]).astype(jnp.bfloat16)
    for copy in token_copies:
        copy.wait()
    chunk = 2 * TILE

    for tile, at in enumerate(OWN_TILES):
        mine = slice(tile * TILE, (tile + 1) * TILE)
        own_queries[mine, :] = tok[at * TILE : (at + 1) * TILE, :model]
    result = dot_plain(own_queries[:, :model], whole[:, :inner])
    own_raw[...] = result
    for head in heads:
        lanes = slice(head * HEAD_DIM, (head + 1) * HEAD_DIM)
        own_queries[:, lanes] = (result[:, lanes] * norm_inverse(result[:, lanes]) * q_gain[:, lanes]).astype(jnp.bfloat16)

    def project(step, carry):
        rows = pl.ds(pl.multiple_of(step * chunk, chunk), chunk)
        result = dot_plain(tok[rows, :model], whole[:, inner : 3 * inner])
        for head in heads:
            lanes = slice(head * HEAD_DIM, (head + 1) * HEAD_DIM)
            k_raw = result[:, lanes]
            keys[rows, lanes] = (k_raw * norm_inverse(k_raw) * k_gain[:, lanes]).astype(jnp.bfloat16)
        values[rows, :] = result[:, inner:].astype(jnp.bfloat16)
        valid = tok[rows, model:].astype(jnp.float32)
        deep = jnp.where(lane_index(chunk) == MASK_LANE, MASK_DEPTH, 0.0)
        marks[rows, :] = (valid * deep - deep + side_marks(step * chunk, chunk)).astype(jnp.bfloat16)
        for tile, at in enumerate(OWN_TILES):
            offset = at * TILE % chunk

            @pl.when(step == at * TILE // chunk)
            def keep():
                own_k_raw[tile * TILE : (tile + 1) * TILE, :] = result[offset : offset + TILE, :inner]

        return carry

    lax.fori_loop(0, EXTENDED // chunk, project, 0, unroll=True)
    count = own_keys.shape[0]
    lane = lane_index(count)
    stats = jnp.where(lane == MASK_LANE, 1.0, 0.0)
    query_marks = (stats + side_rows(count)).astype(jnp.bfloat16)
    for head in heads:
        lanes = slice(head * HEAD_DIM, (head + 1) * HEAD_DIM)
        q_aug = jnp.concatenate([own_queries[:, lanes], query_marks], axis=1)
        k_aug = jnp.concatenate([keys[:, lanes], marks[...]], axis=1)
        weights = jnp.exp(dot_rows(q_aug, k_aug) * FACTOR)
        total = jnp.sum(weights, axis=-1, keepdims=True)
        probs = weights * (1.0 / total)
        attended[:, lanes] = dot_plain(probs.astype(jnp.bfloat16), values[:, lanes]).astype(jnp.bfloat16)
        grad_probs = dot_rows(message[:, lanes], values[:, lanes])
        delta = jnp.sum(probs * grad_probs, axis=-1, keepdims=True)
        grad_scores = (probs * (grad_probs - delta)).astype(jnp.bfloat16)
        upstream_q = dot_plain(grad_scores, keys[:, lanes]) * FACTOR
        grad_q[:, lanes] = norm_backward(own_raw[:, lanes], q_gain[:, lanes], upstream_q).astype(jnp.bfloat16)
        for n, part in enumerate(three_parts(jnp.log(total) * (1.0 / FACTOR))):
            stats = jnp.where(lane == 3 * head + n, part, stats)
        for n, part in enumerate(three_parts(delta)):
            stats = jnp.where(lane == 9 + 3 * head + n, part, stats)
    message[:, inner:] = stats.astype(jnp.bfloat16)
    for tile, at in enumerate(OWN_TILES):
        mine = slice(tile * TILE, (tile + 1) * TILE)
        ext = slice(at * TILE, (at + 1) * TILE)
        own_keys[mine, :] = keys[ext, :]
        own_values[mine, :] = values[ext, :]
        own_marks[mine, :] = marks[ext, :]
    whole_copy.wait()


def queries_kernel(place, own, up, down, left, right, shared, whole, q_gain, queries, weight, tok, sems, weight_sem):
    inner = weight.shape[1]
    model = weight.shape[0]
    weight_copy = pltpu.make_async_copy(whole.at[:, pl.ds(0, inner)], weight, weight_sem.at[0])
    copies = token_copies_of(lax.rem(place[0], 2), own, up, down, left, right, shared, tok, sems)
    for copy in [weight_copy] + copies:
        copy.start()
    weight_copy.wait()
    chunk = 4 * TILE
    for step, arrived in enumerate((copies[:3], copies[3:7], copies[7:])):
        for copy in arrived:
            copy.wait()
        rows = slice(step * chunk, (step + 1) * chunk)
        result = dot_plain(tok[rows, :model], weight[...])
        for head in range(inner // HEAD_DIM):
            lanes = slice(head * HEAD_DIM, (head + 1) * HEAD_DIM)
            q_raw = result[:, lanes]
            queries[rows, lanes] = (q_raw * norm_inverse(q_raw) * q_gain[:, lanes]).astype(jnp.bfloat16)


def back_kernel(place, own, up, down, left, right, queries, keys, values, marks, k_raw, grad_q, whole, k_gain,
                kept, sent, ext, grad_qkv, weight, sems, weight_sem):
    inner = queries.shape[1]
    copies = extended_copies(own, up, down, left, right, ext, sems)
    weight_copy = pltpu.make_async_copy(whole.at[:, pl.ds(0, 3 * inner)], weight, weight_sem.at[0])
    for copy in copies + [weight_copy]:
        copy.start()
    for copy in copies:
        copy.wait()
    grad_qkv[:, :inner] = grad_q[...]
    count = keys.shape[0]
    lane = lane_index(count)
    stats = ext[:, inner:] + side_marks(0, EXTENDED).astype(jnp.bfloat16)
    key_marks = marks[...] + side_rows(count).astype(jnp.bfloat16)
    for head in range(inner // HEAD_DIM):
        lanes = slice(head * HEAD_DIM, (head + 1) * HEAD_DIM)
        k_signs = jnp.where((lane >= 3 * head) & (lane < 3 * head + 3), -1.0, 0.0).astype(jnp.bfloat16)
        v_signs = jnp.where((lane >= 9 + 3 * head) & (lane < 12 + 3 * head), -1.0, 0.0).astype(jnp.bfloat16)
        k_aug = jnp.concatenate([keys[:, lanes], key_marks + k_signs], axis=1)
        v_aug = jnp.concatenate([values[:, lanes], v_signs], axis=1)
        probs = jnp.exp(dot_rows(k_aug, jnp.concatenate([queries[:, lanes], stats], axis=1)) * FACTOR)
        centred = dot_rows(v_aug, jnp.concatenate([ext[:, lanes], stats], axis=1))
        grad_scores = (probs * centred).astype(jnp.bfloat16)
        grad_v = dot_plain(probs.astype(jnp.bfloat16), ext[:, lanes])
        upstream_k = dot_plain(grad_scores, queries[:, lanes]) * FACTOR
        grad_k = norm_backward(k_raw[:, lanes], k_gain[:, lanes], upstream_k)
        grad_qkv[:, inner + head * HEAD_DIM : inner + (head + 1) * HEAD_DIM] = grad_k.astype(jnp.bfloat16)
        grad_qkv[:, 2 * inner + head * HEAD_DIM : 2 * inner + (head + 1) * HEAD_DIM] = grad_v.astype(jnp.bfloat16)
    weight_copy.wait()
    half = kept.shape[1]
    for target, group in ((sent, 1 - place[1]), (kept, place[1])):
        rows = pl.ds(pl.multiple_of(group * half, half), half)
        target[...] = dot_rows(grad_qkv[...], weight[rows, :]).astype(jnp.bfloat16)


def steps(axis, shift, wrap=False):
    count = lax.axis_size(axis)
    return [(i, (i + shift) % count) for i in range(count) if wrap or 0 <= i + shift < count]


def spread_height(own):
    up = lax.ppermute(own, "height", steps("height", 1))
    down = lax.ppermute(own, "height", steps("height", -1))
    return up, down


def spread_width(first, last):
    left = lax.ppermute(last, "width", steps("width", 1))
    right = lax.ppermute(first, "width", steps("width", -1))
    return left, right


def joined_columns(up, own, down):
    return [jnp.concatenate([part[i * TILE : (i + 1) * TILE] for part in (up, own, down)], axis=0) for i in (0, 1)]


def flip(x, bit):
    count = lax.axis_size("height")
    return lax.ppermute(x, "height", [(i, i ^ bit) for i in range(count)])


def gather_height(block, place, up, own, down):
    shift = lambda x, by: lax.ppermute(x, "height", steps("height", by, True))
    rows = block.shape[0]
    pair = jnp.concatenate([block, flip(block, 2)], axis=0)
    pair, first, last = lax.optimization_barrier((pair, *columns(place, up, own, down)))
    left, right = spread_width(first, last)
    core = place[0] & 1
    give = lambda part: lax.dynamic_slice(part, ((1 - core) * TILE, 0), (TILE, part.shape[1]))
    shared = flip(jnp.concatenate([give(left), give(right)], axis=0), 1)
    north, south = shift(pair, 4), shift(pair, -4)
    far, far_beside = shift(north[:rows], 4), shift(south[rows:], -4)
    near = jnp.concatenate([pair, north, south], axis=0)
    near, far = lax.optimization_barrier((near, far))
    far = jnp.concatenate([far, far_beside], axis=0)
    return [near, far, flip(near, 1), flip(far, 1)], left, right, shared


def columns_kernel(place, up, own, down, first, last, sems):
    def copy_all(upper, lower):
        copies = [
            pltpu.make_async_copy(part.at[pl.ds(side * TILE, TILE)], target.at[pl.ds(n * TILE, TILE)], sems.at[2 * side + n])
            for side, target in enumerate((first, last))
            for n, part in enumerate((upper, lower))
        ]
        for copy in copies:
            copy.start()
        for copy in copies:
            copy.wait()

    @pl.when(place[0] % 2 == 0)
    def even():
        copy_all(up, own)

    @pl.when(place[0] % 2 == 1)
    def odd():
        copy_all(own, down)


def columns(place, up, own, down):
    anywhere = pl.BlockSpec(memory_space=pl.ANY)
    out = jax.ShapeDtypeStruct((2 * TILE, own.shape[1]), own.dtype)
    return pl.pallas_call(
        columns_kernel,
        out_shape=(out, out),
        in_specs=[pl.BlockSpec(memory_space=pltpu.SMEM)] + [anywhere] * 3,
        out_specs=(whole_spec(), whole_spec()),
        scratch_shapes=[pltpu.SemaphoreType.DMA((4,))],
        compiler_params=pltpu.CompilerParams(vmem_limit_bytes=VMEM_BYTES),
        name="columns",
    )(place, up, own, down)


def whole_spec():
    return pl.BlockSpec(memory_space=pltpu.VMEM)


def on_device(tokens, grad_out, qkv_weight, out_weight, q_gain, k_gain, key_valid):
    model = tokens.shape[-1]
    inner = q_gain.shape[0]
    count = tokens.shape[0] * tokens.shape[1] * tokens.shape[2]
    shard_rows = qkv_weight.shape[0]
    place = jnp.stack([lax.axis_index("height"), lax.axis_index("head")]).astype(jnp.int32)
    valid = key_valid.reshape(count, 1).astype(jnp.bfloat16)
    marked = jnp.concatenate([tokens.reshape(count, model), jnp.broadcast_to(valid, (count, LANES))], axis=1)
    up, down = spread_height(marked)
    joined = jnp.concatenate([qkv_weight.reshape(shard_rows, 3 * inner), out_weight], axis=1)
    along_width = lax.all_gather(joined, "width", axis=0, tiled=True)
    along_width, up, down = lax.optimization_barrier((along_width, up, down))
    blocks, left, right, shared = gather_height(along_width, place, up, marked, down)
    q_gains, k_gains = q_gain.reshape(1, inner), k_gain.reshape(1, inner)
    anywhere = pl.BlockSpec(memory_space=pl.ANY)
    shape = jax.ShapeDtypeStruct
    half = jnp.bfloat16
    whole, keys, values, marks, k_raw, grad_q, attended, message = pl.pallas_call(
        front_kernel,
        out_shape=(
            shape((model, 4 * inner), half),
            shape((count, inner), half),
            shape((count, inner), half),
            shape((count, LANES), half),
            shape((count, inner), jnp.float32),
            shape((count, inner), half),
            shape((count, inner), half),
            shape((count, inner + LANES), half),
        ),
        in_specs=[pl.BlockSpec(memory_space=pltpu.SMEM)] + [anywhere] * 11 + [whole_spec()] * 2,
        out_specs=(anywhere,) + tuple(whole_spec() for _ in range(7)),
        scratch_shapes=[
            pltpu.VMEM((model, 4 * inner), half),
            pltpu.VMEM((EXTENDED, model + LANES), half),
            pltpu.VMEM((count, model), half),
            pltpu.VMEM((EXTENDED, inner), half),
            pltpu.VMEM((EXTENDED, inner), half),
            pltpu.VMEM((EXTENDED, LANES), half),
            pltpu.VMEM((count, inner), jnp.float32),
            pltpu.VMEM((count, model), half),
            pltpu.SemaphoreType.DMA((10,)),
            pltpu.SemaphoreType.DMA((16,)),
            pltpu.SemaphoreType.DMA((1,)),
            pltpu.SemaphoreType.DMA((1,)),
        ],
        compiler_params=pltpu.CompilerParams(vmem_limit_bytes=VMEM_BYTES),
        name="front",
    )(place, marked, up, down, left, right, shared, grad_out.reshape(count, model), *blocks, q_gains, k_gains)

    group = lax.axis_index("head")
    width = model // 2
    swap = lambda x: lax.ppermute(x, "head", [(0, 1), (1, 0)])
    part = lambda which: lax.dynamic_slice(whole, (which * width, 3 * inner), (width, inner))
    beyond = (marked, up, down, left, right, shared)
    up, down = spread_height(message)
    mixed_sent = dot_rows(attended, part(1 - group)).astype(half)
    up, down, mixed_sent = lax.optimization_barrier((up, down, mixed_sent))
    mixed_kept = dot_rows(attended, part(group)).astype(half)
    mixed_got = swap(mixed_sent)
    left, right = spread_width(*joined_columns(up, message, down))
    up, *beyond = lax.optimization_barrier((up, *beyond))
    queries = pl.pallas_call(
        queries_kernel,
        out_shape=shape((EXTENDED, inner), half),
        in_specs=[pl.BlockSpec(memory_space=pltpu.SMEM)] + [anywhere] * 7 + [whole_spec()],
        out_specs=whole_spec(),
        scratch_shapes=[
            pltpu.VMEM((model, inner), half),
            pltpu.VMEM((EXTENDED, model + LANES), half),
            pltpu.SemaphoreType.DMA((10,)),
            pltpu.SemaphoreType.DMA((1,)),
        ],
        compiler_params=pltpu.CompilerParams(vmem_limit_bytes=VMEM_BYTES),
        cost_estimate=pl.CostEstimate(flops=2 * EXTENDED * model * inner, bytes_accessed=8 * 2**20, transcendentals=0),
        name="queries",
    )(place, *beyond, whole, q_gains)
    kept, sent = pl.pallas_call(
        back_kernel,
        out_shape=(shape((count, width), half), shape((count, width), half)),
        in_specs=[pl.BlockSpec(memory_space=pltpu.SMEM)] + [anywhere] * 5 + [whole_spec()] * 6 + [anywhere, whole_spec()],
        out_specs=(whole_spec(), whole_spec()),
        scratch_shapes=[
            pltpu.VMEM((EXTENDED, inner + LANES), half),
            pltpu.VMEM((count, 3 * inner), half),
            pltpu.VMEM((model, 3 * inner), half),
            pltpu.SemaphoreType.DMA((8,)),
            pltpu.SemaphoreType.DMA((1,)),
        ],
        compiler_params=pltpu.CompilerParams(vmem_limit_bytes=VMEM_BYTES),
        name="back",
    )(place, message, up, down, left, right, queries, keys, values, marks, k_raw, grad_q, whole, k_gains)
    total = lambda a, b: (a.astype(jnp.float32) + b.astype(jnp.float32)).astype(half)
    mixed = total(mixed_kept, mixed_got)
    grad_in = total(kept, swap(sent))
    out_shape = tokens.shape[:3] + (width,)
    return (mixed.reshape(out_shape), grad_in.reshape(out_shape))


def solution(mesh):
    placed = (
        P("height", "width", None, None),
        P("height", "width", None, None),
        P(("height", "width"), None, "head"),
        P(("height", "width"), "head"),
        P("head"),
        P("head"),
        P("height", "width", None),
    )
    return jax.shard_map(
        on_device,
        mesh=mesh,
        in_specs=placed,
        out_specs=(P("height", "width", None, "head"), P("height", "width", None, "head")),
        check_vma=False,
    )
```

```python
import functools

import jax
import jax.numpy as jnp
from jax import lax
from jax.experimental import pallas as pl
from jax.experimental.pallas import tpu as pltpu
from jax.sharding import PartitionSpec as P

HEAD_DIM = 128
LANES = 128
TILE = 144
COLUMN = 3 * TILE
WINDOW = 9 * TILE
EXTENDED = 12 * TILE
OWN_TILES = (4, 7)
MASK_LANE = 18
SIDE_LANES = (19, 20)
MASK_DEPTH = 1e5
FACTOR = HEAD_DIM ** (-0.5)
VMEM_BYTES = 50 * 1024 * 1024
epsilon = 1e-06


def dot_rows(left, right):
    return lax.dot_general(left, right, (((1,), (1,)), ((), ())), preferred_element_type=jnp.float32)


def dot_plain(left, right):
    return jnp.dot(left, right, preferred_element_type=jnp.float32)


def lane_index(rows):
    return lax.broadcasted_iota(jnp.int32, (rows, LANES), 1)


def side_rows(rows):
    row = lax.broadcasted_iota(jnp.int32, (rows, LANES), 0)
    lane = lane_index(rows)
    first = (row < TILE) & (lane == SIDE_LANES[0])
    second = (row >= TILE) & (lane == SIDE_LANES[1])
    return jnp.where(first | second, 1.0, 0.0)


def side_marks(start, rows):
    row = start + lax.broadcasted_iota(jnp.int32, (rows, LANES), 0)
    lane = lane_index(rows)
    last = (row >= WINDOW) & (lane == SIDE_LANES[0])
    first = (row < COLUMN) & (lane == SIDE_LANES[1])
    return jnp.where(first | last, -MASK_DEPTH, 0.0)


def norm_inverse(raw_values):
    return lax.rsqrt(jnp.mean(raw_values * raw_values, axis=-1, keepdims=True) + epsilon)


def norm_backward(raw_values, gain_vec, upstream):
    inverse = norm_inverse(raw_values)
    weighted = gain_vec * upstream
    inner_mean = jnp.mean(weighted * raw_values, axis=-1, keepdims=True)
    return inverse * weighted - raw_values * (inverse * inverse * inverse) * inner_mean


def three_parts(values):
    first = values.astype(jnp.bfloat16)
    rest = values - first.astype(jnp.float32)
    second = rest.astype(jnp.bfloat16)
    third = (rest - second.astype(jnp.float32)).astype(jnp.bfloat16)
    return [part.astype(jnp.float32) for part in (first, second, third)]


def extended_copies(own, up, down, left, right, target, sems):
    tile = lambda ref, i: ref.at[pl.ds(i * TILE, TILE)]
    pairs = [
        (left, 0, 3),
        (tile(up, 0), 3, 1),
        (tile(own, 0), 4, 1),
        (tile(down, 0), 5, 1),
        (tile(up, 1), 6, 1),
        (tile(own, 1), 7, 1),
        (tile(down, 1), 8, 1),
        (right, 9, 3),
    ]
    return [
        pltpu.make_async_copy(src, target.at[pl.ds(at * TILE, count * TILE)], sems.at[n])
        for n, (src, at, count) in enumerate(pairs)
    ]


def token_copies_of(core, own, up, down, left, right, shared, target, sems):
    pairs = [
        (left, 0, 2, core),
        (shared, 0, 1, 2 - 2 * core),
        (up, 0, 1, 3),
        (own, 0, 1, 4),
        (down, 0, 1, 5),
        (up, 1, 1, 6),
        (own, 1, 1, 7),
        (down, 1, 1, 8),
        (right, 0, 2, 9 + core),
        (shared, 1, 1, 11 - 2 * core),
    ]
    return [
        pltpu.make_async_copy(
            src.at[pl.ds(first * TILE, count * TILE)],
            target.at[pl.ds(pl.multiple_of(at * TILE, TILE), count * TILE)],
            sems.at[n],
        )
        for n, (src, first, count, at) in enumerate(pairs)
    ]


def front_kernel(place, own, up, down, left, right, shared, upstream, *rest):
    pieces, rest = rest[:4], rest[4:]
    (q_gain, k_gain, whole_out, own_keys, own_values, own_marks, own_k_raw, grad_q, attended, message,
     whole, tok, grad, keys, values, marks, own_raw, own_queries, token_sems, block_sems, grad_sem, whole_sem) = rest
    here = place[0]
    north, south = lax.rem(here + 12, 16), lax.rem(here + 4, 16)
    far = lax.rem(here + 8, 16)
    near = [here, here ^ 2, north, north ^ 2, south, south ^ 2]
    spots = [near, [far, far ^ 2], [spot ^ 1 for spot in near], [far ^ 1, far ^ 3]]
    parts = [(piece, n, spot) for piece, some in zip(pieces, spots) for n, spot in enumerate(some)]
    block_copies = [
        pltpu.make_async_copy(
            piece.at[pl.ds(n * 96, 96)], whole.at[pl.ds(pl.multiple_of(spot * 96, 96), 96)], block_sems.at[i]
        )
        for i, (piece, n, spot) in enumerate(parts)
    ]
    grad_copy = pltpu.make_async_copy(upstream, grad, grad_sem.at[0])
    token_copies = token_copies_of(lax.rem(here, 2), own, up, down, left, right, shared, tok, token_sems)
    whole_copy = pltpu.make_async_copy(whole, whole_out, whole_sem.at[0])
    for copy in block_copies + [grad_copy] + token_copies[3:7] + token_copies[:3] + token_copies[7:]:
        copy.start()
    for copy in block_copies + [grad_copy]:
        copy.wait()
    whole_copy.start()
    inner = own_keys.shape[1]
    heads = range(inner // HEAD_DIM)
    model = whole.shape[0]
    message[:, :inner] = dot_plain(grad[...], whole[:, 3 * inner :]).astype(jnp.bfloat16)
    for copy in token_copies[3:7]:
        copy.wait()
    chunk = 4 * TILE
    for tile, at in enumerate(OWN_TILES):
        mine = slice(tile * TILE, (tile + 1) * TILE)
        own_queries[mine, :] = tok[at * TILE : (at + 1) * TILE, :model]
    result = dot_plain(own_queries[:, :model], whole[:, :inner])
    own_raw[...] = result
    for head in heads:
        lanes = slice(head * HEAD_DIM, (head + 1) * HEAD_DIM)
        own_queries[:, lanes] = (result[:, lanes] * norm_inverse(result[:, lanes]) * q_gain[:, lanes]).astype(jnp.bfloat16)

    for step, arrived in ((1, []), (0, token_copies[:3]), (2, token_copies[7:])):
        for copy in arrived:
            copy.wait()
        rows = slice(step * chunk, (step + 1) * chunk)
        result = dot_plain(tok[rows, :model], whole[:, inner : 3 * inner])
        for head in heads:
            lanes = slice(head * HEAD_DIM, (head + 1) * HEAD_DIM)
            k_raw = result[:, lanes]
            keys[rows, lanes] = (k_raw * norm_inverse(k_raw) * k_gain[:, lanes]).astype(jnp.bfloat16)
        values[rows, :] = result[:, inner:].astype(jnp.bfloat16)
        valid = tok[rows, model:].astype(jnp.float32)
        deep = jnp.where(lane_index(chunk) == MASK_LANE, MASK_DEPTH, 0.0)
        marks[rows, :] = (valid * deep - deep + side_marks(step * chunk, chunk)).astype(jnp.bfloat16)
        for tile, at in enumerate(OWN_TILES):
            if at * TILE // chunk == step:
                offset = at * TILE % chunk
                own_k_raw[tile * TILE : (tile + 1) * TILE, :] = result[offset : offset + TILE, :inner]

    count = own_keys.shape[0]
    lane = lane_index(count)
    stats = jnp.where(lane == MASK_LANE, 1.0, 0.0)
    query_marks = (stats + side_rows(count)).astype(jnp.bfloat16)
    for head in heads:
        lanes = slice(head * HEAD_DIM, (head + 1) * HEAD_DIM)
        q_aug = jnp.concatenate([own_queries[:, lanes], query_marks], axis=1)
        k_aug = jnp.concatenate([keys[:, lanes], marks[...]], axis=1)
        weights = jnp.exp(dot_rows(q_aug, k_aug) * FACTOR)
        total = jnp.sum(weights, axis=-1, keepdims=True)
        probs = weights * (1.0 / total)
        attended[:, lanes] = dot_plain(probs.astype(jnp.bfloat16), values[:, lanes]).astype(jnp.bfloat16)
        grad_probs = dot_rows(message[:, lanes], values[:, lanes])
        delta = jnp.sum(probs * grad_probs, axis=-1, keepdims=True)
        grad_scores = (probs * (grad_probs - delta)).astype(jnp.bfloat16)
        upstream_q = dot_plain(grad_scores, keys[:, lanes]) * FACTOR
        grad_q[:, lanes] = norm_backward(own_raw[:, lanes], q_gain[:, lanes], upstream_q).astype(jnp.bfloat16)
        for n, part in enumerate(three_parts(jnp.log(total) * (1.0 / FACTOR))):
            stats = jnp.where(lane == 3 * head + n, part, stats)
        for n, part in enumerate(three_parts(delta)):
            stats = jnp.where(lane == 9 + 3 * head + n, part, stats)
    message[:, inner:] = stats.astype(jnp.bfloat16)
    for tile, at in enumerate(OWN_TILES):
        mine = slice(tile * TILE, (tile + 1) * TILE)
        ext = slice(at * TILE, (at + 1) * TILE)
        own_keys[mine, :] = keys[ext, :]
        own_values[mine, :] = values[ext, :]
        own_marks[mine, :] = marks[ext, :]
    whole_copy.wait()


def queries_kernel(place, own, up, down, left, right, shared, whole, q_gain, queries, weight, tok, sems, weight_sem):
    inner = weight.shape[1]
    model = weight.shape[0]
    weight_copy = pltpu.make_async_copy(whole.at[:, pl.ds(0, inner)], weight, weight_sem.at[0])
    copies = token_copies_of(lax.rem(place[0], 2), own, up, down, left, right, shared, tok, sems)
    for copy in [weight_copy] + copies:
        copy.start()
    weight_copy.wait()
    chunk = 4 * TILE
    for step, arrived in enumerate((copies[:3], copies[3:7], copies[7:])):
        for copy in arrived:
            copy.wait()
        rows = slice(step * chunk, (step + 1) * chunk)
        result = dot_plain(tok[rows, :model], weight[...])
        for head in range(inner // HEAD_DIM):
            lanes = slice(head * HEAD_DIM, (head + 1) * HEAD_DIM)
            q_raw = result[:, lanes]
            queries[rows, lanes] = (q_raw * norm_inverse(q_raw) * q_gain[:, lanes]).astype(jnp.bfloat16)


def back_kernel(place, own, up, down, left, right, queries, keys, values, marks, k_raw, grad_q, whole, k_gain,
                kept, sent, ext, grad_qkv, weight, sems, weight_sem):
    inner = queries.shape[1]
    copies = extended_copies(own, up, down, left, right, ext, sems)
    weight_copy = pltpu.make_async_copy(whole.at[:, pl.ds(0, 3 * inner)], weight, weight_sem.at[0])
    for copy in copies + [weight_copy]:
        copy.start()
    for copy in copies:
        copy.wait()
    grad_qkv[:, :inner] = grad_q[...]
    count = keys.shape[0]
    lane = lane_index(count)
    stats = ext[:, inner:] + side_marks(0, EXTENDED).astype(jnp.bfloat16)
    key_marks = marks[...] + side_rows(count).astype(jnp.bfloat16)
    for head in range(inner // HEAD_DIM):
        lanes = slice(head * HEAD_DIM, (head + 1) * HEAD_DIM)
        k_signs = jnp.where((lane >= 3 * head) & (lane < 3 * head + 3), -1.0, 0.0).astype(jnp.bfloat16)
        v_signs = jnp.where((lane >= 9 + 3 * head) & (lane < 12 + 3 * head), -1.0, 0.0).astype(jnp.bfloat16)
        k_aug = jnp.concatenate([keys[:, lanes], key_marks + k_signs], axis=1)
        v_aug = jnp.concatenate([values[:, lanes], v_signs], axis=1)
        probs = jnp.exp(dot_rows(k_aug, jnp.concatenate([queries[:, lanes], stats], axis=1)) * FACTOR)
        centred = dot_rows(v_aug, jnp.concatenate([ext[:, lanes], stats], axis=1))
        grad_scores = (probs * centred).astype(jnp.bfloat16)
        grad_v = dot_plain(probs.astype(jnp.bfloat16), ext[:, lanes])
        upstream_k = dot_plain(grad_scores, queries[:, lanes]) * FACTOR
        grad_k = norm_backward(k_raw[:, lanes], k_gain[:, lanes], upstream_k)
        grad_qkv[:, inner + head * HEAD_DIM : inner + (head + 1) * HEAD_DIM] = grad_k.astype(jnp.bfloat16)
        grad_qkv[:, 2 * inner + head * HEAD_DIM : 2 * inner + (head + 1) * HEAD_DIM] = grad_v.astype(jnp.bfloat16)
    weight_copy.wait()
    half = kept.shape[1]
    for target, group in ((sent, 1 - place[1]), (kept, place[1])):
        rows = pl.ds(pl.multiple_of(group * half, half), half)
        target[...] = dot_rows(grad_qkv[...], weight[rows, :]).astype(jnp.bfloat16)


def steps(axis, shift, wrap=False):
    count = lax.axis_size(axis)
    return [(i, (i + shift) % count) for i in range(count) if wrap or 0 <= i + shift < count]


def spread_height(own):
    up = lax.ppermute(own, "height", steps("height", 1))
    down = lax.ppermute(own, "height", steps("height", -1))
    return up, down


def spread_width(first, last):
    left = lax.ppermute(last, "width", steps("width", 1))
    right = lax.ppermute(first, "width", steps("width", -1))
    return left, right


def joined_columns(up, own, down):
    return [jnp.concatenate([part[i * TILE : (i + 1) * TILE] for part in (up, own, down)], axis=0) for i in (0, 1)]


def flip(x, bit):
    count = lax.axis_size("height")
    return lax.ppermute(x, "height", [(i, i ^ bit) for i in range(count)])


def gather_height(block, place, up, own, down):
    shift = lambda x, by: lax.ppermute(x, "height", steps("height", by, True))
    rows = block.shape[0]
    pair = jnp.concatenate([block, flip(block, 2)], axis=0)
    pair, first, last = lax.optimization_barrier((pair, *columns(place, up, own, down)))
    north, south = shift(pair, 4), shift(pair, -4)
    far, far_beside = shift(north[:rows], 4), shift(south[rows:], -4)
    left, right = spread_width(first, last)
    core = place[0] & 1
    give = lambda part: lax.dynamic_slice(part, ((1 - core) * TILE, 0), (TILE, part.shape[1]))
    shared = flip(jnp.concatenate([give(left), give(right)], axis=0), 1)
    near = jnp.concatenate([pair, north, south], axis=0)
    near, far = lax.optimization_barrier((near, far))
    far = jnp.concatenate([far, far_beside], axis=0)
    return [near, far, flip(near, 1), flip(far, 1)], left, right, shared


def columns_kernel(place, up, own, down, first, last, sems):
    def copy_all(upper, lower):
        copies = [
            pltpu.make_async_copy(part.at[pl.ds(side * TILE, TILE)], target.at[pl.ds(n * TILE, TILE)], sems.at[2 * side + n])
            for side, target in enumerate((first, last))
            for n, part in enumerate((upper, lower))
        ]
        for copy in copies:
            copy.start()
        for copy in copies:
            copy.wait()

    @pl.when(place[0] % 2 == 0)
    def even():
        copy_all(up, own)

    @pl.when(place[0] % 2 == 1)
    def odd():
        copy_all(own, down)


def columns(place, up, own, down):
    anywhere = pl.BlockSpec(memory_space=pl.ANY)
    out = jax.ShapeDtypeStruct((2 * TILE, own.shape[1]), own.dtype)
    return pl.pallas_call(
        columns_kernel,
        out_shape=(out, out),
        in_specs=[pl.BlockSpec(memory_space=pltpu.SMEM)] + [anywhere] * 3,
        out_specs=(whole_spec(), whole_spec()),
        scratch_shapes=[pltpu.SemaphoreType.DMA((4,))],
        compiler_params=pltpu.CompilerParams(vmem_limit_bytes=VMEM_BYTES),
        name="columns",
    )(place, up, own, down)


def whole_spec():
    return pl.BlockSpec(memory_space=pltpu.VMEM)


def on_device(tokens, grad_out, qkv_weight, out_weight, q_gain, k_gain, key_valid):
    model = tokens.shape[-1]
    inner = q_gain.shape[0]
    count = tokens.shape[0] * tokens.shape[1] * tokens.shape[2]
    shard_rows = qkv_weight.shape[0]
    place = jnp.stack([lax.axis_index("height"), lax.axis_index("head")]).astype(jnp.int32)
    valid = key_valid.reshape(count, 1).astype(jnp.bfloat16)
    marked = jnp.concatenate([tokens.reshape(count, model), jnp.broadcast_to(valid, (count, LANES))], axis=1)
    up, down = spread_height(marked)
    joined = jnp.concatenate([qkv_weight.reshape(shard_rows, 3 * inner), out_weight], axis=1)
    along_width = lax.all_gather(joined, "width", axis=0, tiled=True)
    along_width, up, down = lax.optimization_barrier((along_width, up, down))
    blocks, left, right, shared = gather_height(along_width, place, up, marked, down)
    q_gains, k_gains = q_gain.reshape(1, inner), k_gain.reshape(1, inner)
    anywhere = pl.BlockSpec(memory_space=pl.ANY)
    shape = jax.ShapeDtypeStruct
    half = jnp.bfloat16
    whole, keys, values, marks, k_raw, grad_q, attended, message = pl.pallas_call(
        front_kernel,
        out_shape=(
            shape((model, 4 * inner), half),
            shape((count, inner), half),
            shape((count, inner), half),
            shape((count, LANES), half),
            shape((count, inner), jnp.float32),
            shape((count, inner), half),
            shape((count, inner), half),
            shape((count, inner + LANES), half),
        ),
        in_specs=[pl.BlockSpec(memory_space=pltpu.SMEM)] + [anywhere] * 11 + [whole_spec()] * 2,
        out_specs=(anywhere,) + tuple(whole_spec() for _ in range(7)),
        scratch_shapes=[
            pltpu.VMEM((model, 4 * inner), half),
            pltpu.VMEM((EXTENDED, model + LANES), half),
            pltpu.VMEM((count, model), half),
            pltpu.VMEM((EXTENDED, inner), half),
            pltpu.VMEM((EXTENDED, inner), half),
            pltpu.VMEM((EXTENDED, LANES), half),
            pltpu.VMEM((count, inner), jnp.float32),
            pltpu.VMEM((count, model), half),
            pltpu.SemaphoreType.DMA((10,)),
            pltpu.SemaphoreType.DMA((16,)),
            pltpu.SemaphoreType.DMA((1,)),
            pltpu.SemaphoreType.DMA((1,)),
        ],
        compiler_params=pltpu.CompilerParams(vmem_limit_bytes=VMEM_BYTES),
        name="front",
    )(place, marked, up, down, left, right, shared, grad_out.reshape(count, model), *blocks, q_gains, k_gains)

    group = lax.axis_index("head")
    width = model // 2
    swap = lambda x: lax.ppermute(x, "head", [(0, 1), (1, 0)])
    part = lambda which: lax.dynamic_slice(whole, (which * width, 3 * inner), (width, inner))
    beyond = (marked, up, down, left, right, shared)
    up, down = spread_height(message)
    mixed_sent = dot_rows(attended, part(1 - group)).astype(half)
    up, down, mixed_sent = lax.optimization_barrier((up, down, mixed_sent))
    mixed_kept = dot_rows(attended, part(group)).astype(half)
    mixed_got = swap(mixed_sent)
    left, right = spread_width(*joined_columns(up, message, down))
    up, *beyond = lax.optimization_barrier((up, *beyond))
    queries = pl.pallas_call(
        queries_kernel,
        out_shape=shape((EXTENDED, inner), half),
        in_specs=[pl.BlockSpec(memory_space=pltpu.SMEM)] + [anywhere] * 7 + [whole_spec()],
        out_specs=whole_spec(),
        scratch_shapes=[
            pltpu.VMEM((model, inner), half),
            pltpu.VMEM((EXTENDED, model + LANES), half),
            pltpu.SemaphoreType.DMA((10,)),
            pltpu.SemaphoreType.DMA((1,)),
        ],
        compiler_params=pltpu.CompilerParams(vmem_limit_bytes=VMEM_BYTES),
        cost_estimate=pl.CostEstimate(flops=2 * EXTENDED * model * inner, bytes_accessed=8 * 2**20, transcendentals=0),
        name="queries",
    )(place, *beyond, whole, q_gains)
    kept, sent = pl.pallas_call(
        back_kernel,
        out_shape=(shape((count, width), half), shape((count, width), half)),
        in_specs=[pl.BlockSpec(memory_space=pltpu.SMEM)] + [anywhere] * 5 + [whole_spec()] * 6 + [anywhere, whole_spec()],
        out_specs=(whole_spec(), whole_spec()),
        scratch_shapes=[
            pltpu.VMEM((EXTENDED, inner + LANES), half),
            pltpu.VMEM((count, 3 * inner), half),
            pltpu.VMEM((model, 3 * inner), half),
            pltpu.SemaphoreType.DMA((8,)),
            pltpu.SemaphoreType.DMA((1,)),
        ],
        compiler_params=pltpu.CompilerParams(vmem_limit_bytes=VMEM_BYTES),
        name="back",
    )(place, message, up, down, left, right, queries, keys, values, marks, k_raw, grad_q, whole, k_gains)
    total = lambda a, b: (a.astype(jnp.float32) + b.astype(jnp.float32)).astype(half)
    mixed = total(mixed_kept, mixed_got)
    grad_in = total(kept, swap(sent))
    out_shape = tokens.shape[:3] + (width,)
    return (mixed.reshape(out_shape), grad_in.reshape(out_shape))


def solution(mesh):
    placed = (
        P("height", "width", None, None),
        P("height", "width", None, None),
        P(("height", "width"), None, "head"),
        P(("height", "width"), "head"),
        P("head"),
        P("head"),
        P("height", "width", None),
    )
    return jax.shard_map(
        on_device,
        mesh=mesh,
        in_specs=placed,
        out_specs=(P("height", "width", None, "head"), P("height", "width", None, "head")),
        check_vma=False,
    )
```

```python
import functools

import jax
import jax.numpy as jnp
from jax import lax
from jax.experimental import pallas as pl
from jax.experimental.pallas import tpu as pltpu
from jax.sharding import PartitionSpec as P

HEAD_DIM = 128
LANES = 128
TILE = 144
COLUMN = 3 * TILE
WINDOW = 9 * TILE
EXTENDED = 12 * TILE
OWN_TILES = (4, 7)
MASK_LANE = 18
SIDE_LANES = (19, 20)
MASK_DEPTH = 1e5
FACTOR = HEAD_DIM ** (-0.5)
VMEM_BYTES = 50 * 1024 * 1024
epsilon = 1e-06


def dot_rows(left, right):
    return lax.dot_general(left, right, (((1,), (1,)), ((), ())), preferred_element_type=jnp.float32)


def dot_plain(left, right):
    return jnp.dot(left, right, preferred_element_type=jnp.float32)


def lane_index(rows):
    return lax.broadcasted_iota(jnp.int32, (rows, LANES), 1)


def side_rows(rows):
    row = lax.broadcasted_iota(jnp.int32, (rows, LANES), 0)
    lane = lane_index(rows)
    first = (row < TILE) & (lane == SIDE_LANES[0])
    second = (row >= TILE) & (lane == SIDE_LANES[1])
    return jnp.where(first | second, 1.0, 0.0)


def side_marks(start, rows):
    row = start + lax.broadcasted_iota(jnp.int32, (rows, LANES), 0)
    lane = lane_index(rows)
    last = (row >= WINDOW) & (lane == SIDE_LANES[0])
    first = (row < COLUMN) & (lane == SIDE_LANES[1])
    return jnp.where(first | last, -MASK_DEPTH, 0.0)


def norm_inverse(raw_values):
    return lax.rsqrt(jnp.mean(raw_values * raw_values, axis=-1, keepdims=True) + epsilon)


def norm_backward(raw_values, gain_vec, upstream):
    inverse = norm_inverse(raw_values)
    weighted = gain_vec * upstream
    inner_mean = jnp.mean(weighted * raw_values, axis=-1, keepdims=True)
    return inverse * weighted - raw_values * (inverse * inverse * inverse) * inner_mean


def three_parts(values):
    first = values.astype(jnp.bfloat16)
    rest = values - first.astype(jnp.float32)
    second = rest.astype(jnp.bfloat16)
    third = (rest - second.astype(jnp.float32)).astype(jnp.bfloat16)
    return [part.astype(jnp.float32) for part in (first, second, third)]


def extended_copies(own, up, down, left, right, target, sems):
    tile = lambda ref, i: ref.at[pl.ds(i * TILE, TILE)]
    pairs = [
        (left, 0, 3),
        (tile(up, 0), 3, 1),
        (tile(own, 0), 4, 1),
        (tile(down, 0), 5, 1),
        (tile(up, 1), 6, 1),
        (tile(own, 1), 7, 1),
        (tile(down, 1), 8, 1),
        (right, 9, 3),
    ]
    return [
        pltpu.make_async_copy(src, target.at[pl.ds(at * TILE, count * TILE)], sems.at[n])
        for n, (src, at, count) in enumerate(pairs)
    ]


def token_copies_of(core, own, up, down, left, right, shared, target, sems):
    pairs = [
        (left, 0, 2, core),
        (shared, 0, 1, 2 - 2 * core),
        (up, 0, 1, 3),
        (own, 0, 1, 4),
        (down, 0, 1, 5),
        (up, 1, 1, 6),
        (own, 1, 1, 7),
        (down, 1, 1, 8),
        (right, 0, 2, 9 + core),
        (shared, 1, 1, 11 - 2 * core),
    ]
    return [
        pltpu.make_async_copy(
            src.at[pl.ds(first * TILE, count * TILE)],
            target.at[pl.ds(pl.multiple_of(at * TILE, TILE), count * TILE)],
            sems.at[n],
        )
        for n, (src, first, count, at) in enumerate(pairs)
    ]


def front_kernel(place, own, up, down, left, right, shared, upstream, *rest):
    pieces, rest = rest[:4], rest[4:]
    (q_gain, k_gain, whole_out, own_keys, own_values, own_marks, own_k_raw, grad_q, attended, message,
     whole, tok, grad, keys, values, marks, own_raw, own_queries, token_sems, block_sems, grad_sem, whole_sem) = rest
    here = place[0]
    north, south = lax.rem(here + 12, 16), lax.rem(here + 4, 16)
    far = lax.rem(here + 8, 16)
    near = [here, here ^ 2, north, north ^ 2, south, south ^ 2]
    spots = [near, [far, far ^ 2], [spot ^ 1 for spot in near], [far ^ 1, far ^ 3]]
    parts = [(piece, n, spot) for piece, some in zip(pieces, spots) for n, spot in enumerate(some)]
    block_copies = [
        pltpu.make_async_copy(
            piece.at[pl.ds(n * 96, 96)], whole.at[pl.ds(pl.multiple_of(spot * 96, 96), 96)], block_sems.at[i]
        )
        for i, (piece, n, spot) in enumerate(parts)
    ]
    grad_copy = pltpu.make_async_copy(upstream, grad, grad_sem.at[0])
    token_copies = token_copies_of(lax.rem(here, 2), own, up, down, left, right, shared, tok, token_sems)
    whole_copy = pltpu.make_async_copy(whole, whole_out, whole_sem.at[0])
    for copy in block_copies + [grad_copy] + token_copies[3:7] + token_copies[:3] + token_copies[7:]:
        copy.start()
    for copy in block_copies + [grad_copy]:
        copy.wait()
    whole_copy.start()
    inner = own_keys.shape[1]
    heads = range(inner // HEAD_DIM)
    model = whole.shape[0]
    message[:, :inner] = dot_plain(grad[...], whole[:, 3 * inner :]).astype(jnp.bfloat16)
    for copy in token_copies[3:7]:
        copy.wait()
    chunk = 4 * TILE
    for tile, at in enumerate(OWN_TILES):
        mine = slice(tile * TILE, (tile + 1) * TILE)
        own_queries[mine, :] = tok[at * TILE : (at + 1) * TILE, :model]
    result = dot_plain(own_queries[:, :model], whole[:, :inner])
    own_raw[...] = result
    for head in heads:
        lanes = slice(head * HEAD_DIM, (head + 1) * HEAD_DIM)
        own_queries[:, lanes] = (result[:, lanes] * norm_inverse(result[:, lanes]) * q_gain[:, lanes]).astype(jnp.bfloat16)

    for step, arrived in ((1, []), (0, token_copies[:3]), (2, token_copies[7:])):
        for copy in arrived:
            copy.wait()
        rows = slice(step * chunk, (step + 1) * chunk)
        result = dot_plain(tok[rows, :model], whole[:, inner : 3 * inner])
        for head in heads:
            lanes = slice(head * HEAD_DIM, (head + 1) * HEAD_DIM)
            k_raw = result[:, lanes]
            keys[rows, lanes] = (k_raw * norm_inverse(k_raw) * k_gain[:, lanes]).astype(jnp.bfloat16)
        values[rows, :] = result[:, inner:].astype(jnp.bfloat16)
        valid = tok[rows, model:].astype(jnp.float32)
        deep = jnp.where(lane_index(chunk) == MASK_LANE, MASK_DEPTH, 0.0)
        marks[rows, :] = (valid * deep - deep + side_marks(step * chunk, chunk)).astype(jnp.bfloat16)
        for tile, at in enumerate(OWN_TILES):
            if at * TILE // chunk == step:
                offset = at * TILE % chunk
                own_k_raw[tile * TILE : (tile + 1) * TILE, :] = result[offset : offset + TILE, :inner]

    count = own_keys.shape[0]
    lane = lane_index(count)
    stats = jnp.where(lane == MASK_LANE, 1.0, 0.0)
    query_marks = (stats + side_rows(count)).astype(jnp.bfloat16)
    for head in heads:
        lanes = slice(head * HEAD_DIM, (head + 1) * HEAD_DIM)
        q_aug = jnp.concatenate([own_queries[:, lanes], query_marks], axis=1)
        k_aug = jnp.concatenate([keys[:, lanes], marks[...]], axis=1)
        weights = jnp.exp(dot_rows(q_aug, k_aug) * FACTOR)
        total = jnp.sum(weights, axis=-1, keepdims=True)
        probs = weights * (1.0 / total)
        attended[:, lanes] = dot_plain(probs.astype(jnp.bfloat16), values[:, lanes]).astype(jnp.bfloat16)
        grad_probs = dot_rows(message[:, lanes], values[:, lanes])
        delta = jnp.sum(probs * grad_probs, axis=-1, keepdims=True)
        grad_scores = (probs * (grad_probs - delta)).astype(jnp.bfloat16)
        upstream_q = dot_plain(grad_scores, keys[:, lanes]) * FACTOR
        grad_q[:, lanes] = norm_backward(own_raw[:, lanes], q_gain[:, lanes], upstream_q).astype(jnp.bfloat16)
        for n, part in enumerate(three_parts(jnp.log(total) * (1.0 / FACTOR))):
            stats = jnp.where(lane == 3 * head + n, part, stats)
        for n, part in enumerate(three_parts(delta)):
            stats = jnp.where(lane == 9 + 3 * head + n, part, stats)
    message[:, inner:] = stats.astype(jnp.bfloat16)
    for tile, at in enumerate(OWN_TILES):
        mine = slice(tile * TILE, (tile + 1) * TILE)
        ext = slice(at * TILE, (at + 1) * TILE)
        own_keys[mine, :] = keys[ext, :]
        own_values[mine, :] = values[ext, :]
        own_marks[mine, :] = marks[ext, :]
    whole_copy.wait()


def queries_kernel(place, own, up, down, left, right, shared, whole, q_gain, queries, weight, tok, sems, weight_sem):
    inner = weight.shape[1]
    model = weight.shape[0]
    weight_copy = pltpu.make_async_copy(whole.at[:, pl.ds(0, inner)], weight, weight_sem.at[0])
    copies = token_copies_of(lax.rem(place[0], 2), own, up, down, left, right, shared, tok, sems)
    for copy in [weight_copy] + copies:
        copy.start()
    weight_copy.wait()
    chunk = 4 * TILE
    for step, arrived in enumerate((copies[:3], copies[3:7], copies[7:])):
        for copy in arrived:
            copy.wait()
        rows = slice(step * chunk, (step + 1) * chunk)
        result = dot_plain(tok[rows, :model], weight[...])
        for head in range(inner // HEAD_DIM):
            lanes = slice(head * HEAD_DIM, (head + 1) * HEAD_DIM)
            q_raw = result[:, lanes]
            queries[rows, lanes] = (q_raw * norm_inverse(q_raw) * q_gain[:, lanes]).astype(jnp.bfloat16)


def back_kernel(place, own, up, down, left, right, queries, keys, values, marks, k_raw, grad_q, whole, k_gain,
                grad_qkv, sent, ext, weight, sems, weight_sem):
    inner = queries.shape[1]
    copies = extended_copies(own, up, down, left, right, ext, sems)
    half = sent.shape[1]
    other = pl.ds(pl.multiple_of((1 - place[1]) * half, half), half)
    weight_copy = pltpu.make_async_copy(whole.at[other, pl.ds(0, 3 * inner)], weight, weight_sem.at[0])
    for copy in copies + [weight_copy]:
        copy.start()
    for copy in copies:
        copy.wait()
    grad_qkv[:, :inner] = grad_q[...]
    count = keys.shape[0]
    lane = lane_index(count)
    stats = ext[:, inner:] + side_marks(0, EXTENDED).astype(jnp.bfloat16)
    key_marks = marks[...] + side_rows(count).astype(jnp.bfloat16)
    for head in range(inner // HEAD_DIM):
        lanes = slice(head * HEAD_DIM, (head + 1) * HEAD_DIM)
        k_signs = jnp.where((lane >= 3 * head) & (lane < 3 * head + 3), -1.0, 0.0).astype(jnp.bfloat16)
        v_signs = jnp.where((lane >= 9 + 3 * head) & (lane < 12 + 3 * head), -1.0, 0.0).astype(jnp.bfloat16)
        k_aug = jnp.concatenate([keys[:, lanes], key_marks + k_signs], axis=1)
        v_aug = jnp.concatenate([values[:, lanes], v_signs], axis=1)
        probs = jnp.exp(dot_rows(k_aug, jnp.concatenate([queries[:, lanes], stats], axis=1)) * FACTOR)
        centred = dot_rows(v_aug, jnp.concatenate([ext[:, lanes], stats], axis=1))
        grad_scores = (probs * centred).astype(jnp.bfloat16)
        grad_v = dot_plain(probs.astype(jnp.bfloat16), ext[:, lanes])
        upstream_k = dot_plain(grad_scores, queries[:, lanes]) * FACTOR
        grad_k = norm_backward(k_raw[:, lanes], k_gain[:, lanes], upstream_k)
        grad_qkv[:, inner + head * HEAD_DIM : inner + (head + 1) * HEAD_DIM] = grad_k.astype(jnp.bfloat16)
        grad_qkv[:, 2 * inner + head * HEAD_DIM : 2 * inner + (head + 1) * HEAD_DIM] = grad_v.astype(jnp.bfloat16)
    weight_copy.wait()
    sent[...] = dot_rows(grad_qkv[...], weight[...]).astype(jnp.bfloat16)


def steps(axis, shift, wrap=False):
    count = lax.axis_size(axis)
    return [(i, (i + shift) % count) for i in range(count) if wrap or 0 <= i + shift < count]


def spread_height(own):
    up = lax.ppermute(own, "height", steps("height", 1))
    down = lax.ppermute(own, "height", steps("height", -1))
    return up, down


def spread_width(first, last):
    left = lax.ppermute(last, "width", steps("width", 1))
    right = lax.ppermute(first, "width", steps("width", -1))
    return left, right


def joined_columns(up, own, down):
    return [jnp.concatenate([part[i * TILE : (i + 1) * TILE] for part in (up, own, down)], axis=0) for i in (0, 1)]


def flip(x, bit):
    count = lax.axis_size("height")
    return lax.ppermute(x, "height", [(i, i ^ bit) for i in range(count)])


def gather_height(block, place, up, own, down):
    shift = lambda x, by: lax.ppermute(x, "height", steps("height", by, True))
    rows = block.shape[0]
    pair = jnp.concatenate([block, flip(block, 2)], axis=0)
    pair, first, last = lax.optimization_barrier((pair, *columns(place, up, own, down)))
    north, south = shift(pair, 4), shift(pair, -4)
    far, far_beside = shift(north[:rows], 4), shift(south[rows:], -4)
    left, right = spread_width(first, last)
    core = place[0] & 1
    give = lambda part: lax.dynamic_slice(part, ((1 - core) * TILE, 0), (TILE, part.shape[1]))
    shared = flip(jnp.concatenate([give(left), give(right)], axis=0), 1)
    near = jnp.concatenate([pair, north, south], axis=0)
    near, far = lax.optimization_barrier((near, far))
    far = jnp.concatenate([far, far_beside], axis=0)
    return [near, far, flip(near, 1), flip(far, 1)], left, right, shared


def columns_kernel(place, up, own, down, first, last, sems):
    def copy_all(upper, lower):
        copies = [
            pltpu.make_async_copy(part.at[pl.ds(side * TILE, TILE)], target.at[pl.ds(n * TILE, TILE)], sems.at[2 * side + n])
            for side, target in enumerate((first, last))
            for n, part in enumerate((upper, lower))
        ]
        for copy in copies:
            copy.start()
        for copy in copies:
            copy.wait()

    @pl.when(place[0] % 2 == 0)
    def even():
        copy_all(up, own)

    @pl.when(place[0] % 2 == 1)
    def odd():
        copy_all(own, down)


def columns(place, up, own, down):
    anywhere = pl.BlockSpec(memory_space=pl.ANY)
    out = jax.ShapeDtypeStruct((2 * TILE, own.shape[1]), own.dtype)
    return pl.pallas_call(
        columns_kernel,
        out_shape=(out, out),
        in_specs=[pl.BlockSpec(memory_space=pltpu.SMEM)] + [anywhere] * 3,
        out_specs=(whole_spec(), whole_spec()),
        scratch_shapes=[pltpu.SemaphoreType.DMA((4,))],
        compiler_params=pltpu.CompilerParams(vmem_limit_bytes=VMEM_BYTES),
        name="columns",
    )(place, up, own, down)


def whole_spec():
    return pl.BlockSpec(memory_space=pltpu.VMEM)


def on_device(tokens, grad_out, qkv_weight, out_weight, q_gain, k_gain, key_valid):
    model = tokens.shape[-1]
    inner = q_gain.shape[0]
    count = tokens.shape[0] * tokens.shape[1] * tokens.shape[2]
    shard_rows = qkv_weight.shape[0]
    place = jnp.stack([lax.axis_index("height"), lax.axis_index("head")]).astype(jnp.int32)
    valid = key_valid.reshape(count, 1).astype(jnp.bfloat16)
    marked = jnp.concatenate([tokens.reshape(count, model), jnp.broadcast_to(valid, (count, LANES))], axis=1)
    up, down = spread_height(marked)
    joined = jnp.concatenate([qkv_weight.reshape(shard_rows, 3 * inner), out_weight], axis=1)
    along_width = lax.all_gather(joined, "width", axis=0, tiled=True)
    along_width, up, down = lax.optimization_barrier((along_width, up, down))
    blocks, left, right, shared = gather_height(along_width, place, up, marked, down)
    q_gains, k_gains = q_gain.reshape(1, inner), k_gain.reshape(1, inner)
    anywhere = pl.BlockSpec(memory_space=pl.ANY)
    shape = jax.ShapeDtypeStruct
    half = jnp.bfloat16
    whole, keys, values, marks, k_raw, grad_q, attended, message = pl.pallas_call(
        front_kernel,
        out_shape=(
            shape((model, 4 * inner), half),
            shape((count, inner), half),
            shape((count, inner), half),
            shape((count, LANES), half),
            shape((count, inner), jnp.float32),
            shape((count, inner), half),
            shape((count, inner), half),
            shape((count, inner + LANES), half),
        ),
        in_specs=[pl.BlockSpec(memory_space=pltpu.SMEM)] + [anywhere] * 11 + [whole_spec()] * 2,
        out_specs=(anywhere,) + tuple(whole_spec() for _ in range(7)),
        scratch_shapes=[
            pltpu.VMEM((model, 4 * inner), half),
            pltpu.VMEM((EXTENDED, model + LANES), half),
            pltpu.VMEM((count, model), half),
            pltpu.VMEM((EXTENDED, inner), half),
            pltpu.VMEM((EXTENDED, inner), half),
            pltpu.VMEM((EXTENDED, LANES), half),
            pltpu.VMEM((count, inner), jnp.float32),
            pltpu.VMEM((count, model), half),
            pltpu.SemaphoreType.DMA((10,)),
            pltpu.SemaphoreType.DMA((16,)),
            pltpu.SemaphoreType.DMA((1,)),
            pltpu.SemaphoreType.DMA((1,)),
        ],
        compiler_params=pltpu.CompilerParams(vmem_limit_bytes=VMEM_BYTES),
        name="front",
    )(place, marked, up, down, left, right, shared, grad_out.reshape(count, model), *blocks, q_gains, k_gains)

    group = lax.axis_index("head")
    width = model // 2
    swap = lambda x: lax.ppermute(x, "head", [(0, 1), (1, 0)])
    part = lambda which: lax.dynamic_slice(whole, (which * width, 3 * inner), (width, inner))
    beyond = (marked, up, down, left, right, shared)
    up, down = spread_height(message)
    mixed_sent = dot_rows(attended, part(1 - group)).astype(half)
    up, down, mixed_sent = lax.optimization_barrier((up, down, mixed_sent))
    mixed_kept = dot_rows(attended, part(group)).astype(half)
    mixed_got = swap(mixed_sent)
    left, right = spread_width(*joined_columns(up, message, down))
    up, *beyond = lax.optimization_barrier((up, *beyond))
    queries = pl.pallas_call(
        queries_kernel,
        out_shape=shape((EXTENDED, inner), half),
        in_specs=[pl.BlockSpec(memory_space=pltpu.SMEM)] + [anywhere] * 7 + [whole_spec()],
        out_specs=whole_spec(),
        scratch_shapes=[
            pltpu.VMEM((model, inner), half),
            pltpu.VMEM((EXTENDED, model + LANES), half),
            pltpu.SemaphoreType.DMA((10,)),
            pltpu.SemaphoreType.DMA((1,)),
        ],
        compiler_params=pltpu.CompilerParams(vmem_limit_bytes=VMEM_BYTES),
        cost_estimate=pl.CostEstimate(flops=2 * EXTENDED * model * inner, bytes_accessed=8 * 2**20, transcendentals=0),
        name="queries",
    )(place, *beyond, whole, q_gains)
    grad_qkv, sent = pl.pallas_call(
        back_kernel,
        out_shape=(shape((count, 3 * inner), half), shape((count, width), half)),
        in_specs=[pl.BlockSpec(memory_space=pltpu.SMEM)] + [anywhere] * 5 + [whole_spec()] * 6 + [anywhere, whole_spec()],
        out_specs=(whole_spec(), whole_spec()),
        scratch_shapes=[
            pltpu.VMEM((EXTENDED, inner + LANES), half),
            pltpu.VMEM((width, 3 * inner), half),
            pltpu.SemaphoreType.DMA((8,)),
            pltpu.SemaphoreType.DMA((1,)),
        ],
        compiler_params=pltpu.CompilerParams(vmem_limit_bytes=VMEM_BYTES),
        name="back",
    )(place, message, up, down, left, right, queries, keys, values, marks, k_raw, grad_q, whole, k_gains)
    total = lambda a, b: (a.astype(jnp.float32) + b.astype(jnp.float32)).astype(half)
    mixed = total(mixed_kept, mixed_got)
    own_rows = lax.dynamic_slice(whole, (group * width, 0), (width, 3 * inner))
    kept = lax.optimization_barrier(dot_rows(grad_qkv, own_rows).astype(half))
    grad_in = total(kept, swap(sent))
    out_shape = tokens.shape[:3] + (width,)
    return (mixed.reshape(out_shape), grad_in.reshape(out_shape))


def solution(mesh):
    placed = (
        P("height", "width", None, None),
        P("height", "width", None, None),
        P(("height", "width"), None, "head"),
        P(("height", "width"), "head"),
        P("head"),
        P("head"),
        P("height", "width", None),
    )
    return jax.shard_map(
        on_device,
        mesh=mesh,
        in_specs=placed,
        out_specs=(P("height", "width", None, "head"), P("height", "width", None, "head")),
        check_vma=False,
    )
```
